256 devices in a mesh: gx: 16 (over y, x_lo, core), gy: 16 (over z, x_hi).
Axes of the slice: x: 4 (x_hi: 2, x_lo: 2; x = x_hi * 2 + x_lo), y: 4, z: 8, core: 2. Of those that a mesh axis runs over, the one named last changes fastest.
Arguments:
- eigen_block: float32 [16, 128, 256, 128], P(None, 'gx', 'gy'), may hold values from -25 to 25, as said below
- search_dirs: float32 [16, 128, 256, 128], P(None, 'gx', 'gy'), may hold values from -3 to 3
Outputs:
- new_block: float32 [16, 128, 256, 128], P(None, 'gx', 'gy')
- new_search: float32 [16, 128, 256, 128], P(None, 'gx', 'gy')
The draws below stay inside these ranges and needn't reach their ends.
Inputs may be any that keep to these rules, and one draw needn't show every extreme that they name: `eigen_block`: real numbers whose typical size changes along the first grid dimension.
All inputs are finite; a program needn't handle non-finite values.
Results may differ from the reference program's by a relative error of at most 0.0003.
Values sent between devices are 32-bit elements; how exact they have to be, the bound alone decides.
A program may use at most 64 MiB of HBM per device.

```python
import jax
import jax.numpy as jnp
from jax import lax

K = 16
NZ = 128
NU_PRE = 2
NU_POST = 2
NC = 4
NX = 128
NY = 256


def draw_eigen_block(key, part):
    key_base, key_rough = jax.random.split(jax.random.fold_in(key, 11))
    shape = (K, NX, NY, NZ)
    plane = jnp.arange(NX, dtype=jnp.float32) / jnp.float32(max(NX - 1, 1))
    rising = jnp.exp(jnp.log(3.0) * plane)[None, :, None, None]
    rough = jnp.exp(jax.random.uniform(key_rough, shape, jnp.float32, -0.7, 0.7))
    base = jnp.clip(jax.random.normal(key_base, shape, jnp.float32), -4.0, 4.0)
    return base * rough * rising


def block_scale(key, dims, shards, smallest, high):
    level = 1.0
    for position, parts in shards:
        heights = jax.random.uniform(jax.random.fold_in(jax.random.fold_in(key, 6), position), (parts,), jnp.float32, smallest / len(shards), high / len(shards))
        level = level * jnp.repeat(jnp.exp(heights), dims[position] // parts).reshape((-1,) + (1,) * (len(dims) - 1 - position))
    return level


def normal_values(stream_key, dims, deviation, reach, cuts=(), kind=jnp.bfloat16):
    entries = jax.random.normal(stream_key, dims, jnp.float32) * deviation
    if len(cuts) > 0:
        entries = block_scale(stream_key, dims, cuts, -0.22, 0.18) * entries
    return jnp.clip(entries, min=-reach, max=reach).astype(kind)


def setup_inputs(seed: int = 0) -> dict:
    splits = jax.random.split(jax.random.key(seed), 3)
    return {
        "eigen_block": draw_eigen_block(jax.random.fold_in(splits[2], 71), 0),
        "search_dirs": normal_values(splits[1], (K, NX, NY, NZ), 0.5, 3.0, ((1, 16), (2, 16)), jnp.float32),
    }


relax = 1.0 / 9.0
coarse_relax = 1.0 / 36.0
shift_value = 13.0

def stencil(full):
    center = full[..., 1:-1, 1:-1, 1:-1]
    beside = full[..., 2:, 1:-1, 1:-1] + full[..., :-2, 1:-1, 1:-1]
    beside = beside + full[..., 1:-1, 2:, 1:-1] + full[..., 1:-1, :-2, 1:-1]
    beside = beside + full[..., 1:-1, 1:-1, 2:] + full[..., 1:-1, 1:-1, :-2]
    return 6.0 * center - beside

def apply_lap(field):
    return stencil(jnp.pad(field, 1))

def restrict(field):
    sx, sy, sz = field.shape
    return field.reshape(sx // 2, 2, sy // 2, 2, sz // 2, 2).sum(axis=(1, 3, 5))

def prolong(field):
    sx, sy, sz = field.shape
    wide = jnp.broadcast_to(field[:, None, :, None, :, None], (sx, 2, sy, 2, sz, 2))
    return wide.reshape(sx * 2, sy * 2, sz * 2)

def vcycle(resid):
    corr = relax * resid
    for sweep in range(NU_PRE):
        corr = corr + relax * (resid - apply_lap(corr))
    rest = resid - apply_lap(corr)
    coarse_r = restrict(rest)
    coarse = coarse_relax * coarse_r
    for sweep in range(NC - 1):
        coarse = coarse + coarse_relax * (coarse_r - 4.0 * apply_lap(coarse))
    corr = corr + prolong(coarse)
    for sweep in range(NU_POST):
        corr = corr + relax * (resid - apply_lap(corr))
    return corr

def ritz_coef(gram, proj, ncells):
    hp = lax.Precision.HIGHEST
    proj = 0.5 * (proj + proj.T)
    lower = jnp.linalg.cholesky(gram)
    inner = jax.scipy.linalg.solve_triangular(lower, proj, lower=True)
    ritz = jax.scipy.linalg.solve_triangular(lower, inner.T, lower=True)
    ritz = 0.5 * (ritz + ritz.T)
    nbasis = gram.shape[0]
    kcount = nbasis // 3
    filtered = shift_value * jnp.eye(nbasis, dtype=jnp.float32)[:, :kcount] - ritz[:, :kcount]
    small = jnp.linalg.cholesky(jnp.dot(filtered.T, filtered, precision=hp))
    scaled = jax.scipy.linalg.solve_triangular(small, filtered.T, lower=True).T
    coef = jax.scipy.linalg.solve_triangular(lower, scaled, lower=True, trans='T')
    return coef * jnp.sqrt(jnp.float32(ncells))

def reference(eigen_block, search_dirs):
    hp = lax.Precision.HIGHEST
    image_x = lax.map(apply_lap, eigen_block)
    image_p = lax.map(apply_lap, search_dirs)
    numer = lax.optimization_barrier(jnp.sum(eigen_block * image_x, axis=(1, 2, 3)))
    denom = lax.optimization_barrier(jnp.sum(eigen_block * eigen_block, axis=(1, 2, 3)))
    theta = numer / denom
    resid = image_x - theta[:, None, None, None] * eigen_block
    precond = lax.map(vcycle, resid)
    image_w = lax.map(apply_lap, precond)
    basis = jnp.concatenate([eigen_block, precond, search_dirs], axis=0)
    images = jnp.concatenate([image_x, image_w, image_p], axis=0)
    gram = jnp.einsum('kxyz,lxyz->kl', basis, basis, precision=hp)
    proj = jnp.einsum('kxyz,lxyz->kl', images, basis, precision=hp)
    coef = ritz_coef(gram, proj, NX * NY * NZ)
    kcount = eigen_block.shape[0]
    coef_p = jnp.concatenate([jnp.zeros((kcount, kcount), jnp.float32), coef[kcount:]], axis=0)
    new_block = jnp.einsum('lk,lxyz->kxyz', coef, basis, precision=hp)
    new_search = jnp.einsum('lk,lxyz->kxyz', coef_p, basis, precision=hp)
    return (new_block, new_search)
```

```python
import functools

import jax
import jax.numpy as jnp
from jax import lax
from jax.experimental import pallas as pl
from jax.experimental.pallas import tpu as pltpu
from jax.sharding import PartitionSpec as P

MESH = pl.DeviceIdType.MESH
HP = lax.Precision.HIGHEST
F32 = jnp.float32
BF16 = jnp.bfloat16

K = 16
NX, NY, NZ = 8, 16, 128
H = 4
CX, CY = NX // 2, NY // 2
HC = 3
HD = 2
SHIFT = 13.0

DIRS = [(-1, 0), (1, 0), (0, -1), (0, 1), (-1, -1), (-1, 1), (1, -1), (1, 1)]


def masks_of(bits):
    out = [(0, 0)]
    for bx, by in bits:
        out = out + [(x | bx, y | by) for x, y in out]
    return out[1:]


CORE = masks_of([(1, 0)])
PLANE = masks_of([(2, 0), (0, 1), (4, 0), (8, 0)])
DEPTH = masks_of([(0, 2), (0, 4), (0, 8)])


def span(step, layers, size, offset):
    if step == 0:
        return (offset, offset, size)
    first, last = layers
    count = last - first + 1
    if step < 0:
        return (offset + first - 1, offset + size + first - 1, count)
    return (offset + size - last, offset - last, count)


def transfers():
    groups = {}
    groups["x1"] = [("x", d, (1, 1), (1, 1)) for d in range(4)]
    deep = [("x", d, (2, 4), (2, 4)) for d in range(4)]
    for d in range(4, 8):
        deep += [("x", d, (1, 1), (1, 3)), ("x", d, (2, 2), (1, 2)), ("x", d, (3, 3), (1, 1))]
    groups["x4"] = deep
    groups["p1"] = [("p", d, (1, 1), (1, 1)) for d in range(4)]
    rough = [("cr", d, (1, 3), (1, 3)) for d in range(4)]
    for d in range(4, 8):
        rough += [("cr", d, (1, 1), (1, 2)), ("cr", d, (2, 2), (1, 1))]
    groups["cr"] = rough
    groups["e"] = [("e", d, (2, 3), (2, 3)) for d in range(4)] + [("e", d, (1, 2), (1, 2)) for d in range(4, 8)]
    groups["c"] = [("c", d, (1, 2), (1, 2)) for d in range(4)] + [("c", d, (1, 1), (1, 1)) for d in range(4, 8)]
    return groups


GROUPS = transfers()
FIRST = {}
COUNT = 0
for _name in GROUPS:
    FIRST[_name] = COUNT
    COUNT += len(GROUPS[_name])

GEOMETRY = {"x": (NX, NY, H), "p": (NX, NY, 1), "e": (NX, NY, H), "cr": (CX, CY, HC), "c": (CX, CY, HD)}


def tree(parts):
    while len(parts) > 1:
        parts = [parts[i] + parts[i + 1] for i in range(0, len(parts), 2)]
    return parts[0]


def chunks(start, stop, width=4):
    return [(j, min(width, stop - j)) for j in range(start, stop, width)]


def kernel(
    x_hbm, p_hbm, block_hbm, search_hbm,
    x_nat, p_nat, x_ext, p_ext, r_ext, ea, eb, ec, crp, ca, cb, cd, split, out_block, out_search,
    th_mine, th_core, th_plane, th_depth, ar_mine, ar_core, ar_plane, ar_depth, ar_full,
    send_sem, recv_sem, red_send, red_recv, local_sem,
):
    gx, gy = lax.axis_index("gx"), lax.axis_index("gy")
    nx, ny = lax.axis_size("gx"), lax.axis_size("gy")
    core = lax.rem(gx, 2)
    load_x = pltpu.make_async_copy(x_hbm, x_nat, local_sem.at[0])
    load_p = pltpu.make_async_copy(p_hbm, p_nat, local_sem.at[1])
    load_x.start()
    load_p.start()

    buffers = {"x": x_ext, "p": p_ext, "e": ec, "cr": crp, "c": cd}
    lane = lax.broadcasted_iota(jnp.int32, (1, 1, NZ), 2)
    first_z, last_z, even = lane == 0, lane == NZ - 1, lane % 2 == 0

    def exists(d, sign):
        dx, dy = DIRS[d]
        tests = []
        if dx:
            tests.append(gx > 0 if dx * sign < 0 else gx < nx - 1)
        if dy:
            tests.append(gy > 0 if dy * sign < 0 else gy < ny - 1)
        return functools.reduce(jnp.logical_and, tests)

    def copy_of(name, index):
        key, d, rows, cols = GROUPS[name][index]
        dx, dy = DIRS[d]
        sx, sy, offset = GEOMETRY[key]
        rs, rd, rn = span(dx, rows, sx, offset)
        cs, cd_, cn = span(dy, cols, sy, offset)
        buf = buffers[key]
        sem = FIRST[name] + index
        return d, pltpu.make_async_remote_copy(
            src_ref=buf.at[pl.ds(rs, rn), pl.ds(cs, cn)],
            dst_ref=buf.at[pl.ds(rd, rn), pl.ds(cd_, cn)],
            send_sem=send_sem.at[sem],
            recv_sem=recv_sem.at[sem],
            device_id=(gx + dx, gy + dy),
            device_id_type=MESH,
        )

    def send(name):
        for index in range(len(GROUPS[name])):
            d, copy = copy_of(name, index)
            pl.when(exists(d, 1))(copy.start)

    def receive(name):
        for index in range(len(GROUPS[name])):
            d, copy = copy_of(name, index)
            pl.when(exists(d, -1))(copy.wait_recv)

    def sent(name):
        for index in range(len(GROUPS[name])):
            d, copy = copy_of(name, index)
            pl.when(exists(d, 1))(copy.wait_send)

    def exchange(masks, base, source, slots):
        copies = [
            pltpu.make_async_remote_copy(
                src_ref=source,
                dst_ref=slots.at[i],
                send_sem=red_send.at[base + i],
                recv_sem=red_recv.at[base + i],
                device_id=(gx ^ mx, gy ^ my),
                device_id_type=MESH,
            )
            for i, (mx, my) in enumerate(masks)
        ]
        for copy in copies:
            copy.start()
        for copy in copies:
            copy.wait_send()
            copy.wait_recv()

    def clear(ref, rows):
        def row(i, carry):
            ref[i] = jnp.zeros(ref.shape[1:], ref.dtype)
            return carry
        lax.fori_loop(0, rows, row, 0)

    clear(x_ext, NX + 2 * H)
    clear(p_ext, NX + 2)
    clear(ec, NX + 2 * H)
    clear(crp, CX + 2 * HC)
    clear(cd, CX + 2 * HD)

    barrier = pltpu.get_barrier_semaphore()
    expected = 0
    for d in range(8):
        dx, dy = DIRS[d]
        there = exists(d, 1)

        @pl.when(there)
        def _():
            pl.semaphore_signal(barrier, inc=1, device_id=(gx + dx, gy + dy), device_id_type=MESH)

        expected = expected + jnp.where(there, 1, 0)
    partners = CORE + PLANE + DEPTH
    for mx, my in partners:
        pl.semaphore_signal(barrier, inc=1, device_id=(gx ^ mx, gy ^ my), device_id_type=MESH)

    clear(r_ext, NX + 2 * H)
    clear(ea, NX + 2 * H)
    clear(eb, NX + 2 * H)
    clear(ca, CX + 2 * HC)
    clear(cb, CX + 2 * HC)

    def put(cell, row, value):
        high = value.astype(BF16)
        split[cell, pl.ds(row, K)] = high
        split[cell, pl.ds(row + 128, K)] = (value - high.astype(F32)).astype(BF16)

    load_x.wait()

    def bring_x(i, carry):
        for j in range(NY):
            value = x_nat[pl.ds(i * NY + j, K, stride=NX * NY), :]
            x_ext[i + H, j + H] = value
        return carry

    lax.fori_loop(0, NX, bring_x, 0)
    pl.semaphore_wait(barrier, expected + len(partners))
    send("x1")
    send("x4")
    load_p.wait()

    def bring_p(i, carry):
        for j in range(NY):
            p_ext[i + 1, j + 1] = p_nat[pl.ds(i * NY + j, K, stride=NX * NY), :]
        return carry

    lax.fori_loop(0, NX, bring_p, 0)
    send("p1")

    def keep(i, carry):
        for j in range(NY):
            cell = i * NY + j
            put(cell, 0, x_ext[i + H, j + H])
            put(cell, 16, p_ext[i + 1, j + 1])
            split[cell, pl.ds(96, 32)] = jnp.zeros((32, NZ), BF16)
            split[cell, pl.ds(224, 32)] = jnp.zeros((32, NZ), BF16)
        return carry

    lax.fori_loop(0, NX, keep, 0)

    def beside_z(center, step):
        zero = jnp.zeros_like(center)
        if step == 1:
            down = jnp.where(first_z, zero, pltpu.roll(center, 1, 2))
            up = jnp.where(last_z, zero, pltpu.roll(center, NZ - 1, 2))
        else:
            down = jnp.where(lane < 2, zero, pltpu.roll(center, 2, 2))
            up = jnp.where(lane >= NZ - 2, zero, pltpu.roll(center, NZ - 2, 2))
        return down + up

    def around(ref, i, j, n, step=1):
        center = ref[i, pl.ds(j, n)]
        beside = ref[i - 1, pl.ds(j, n)] + ref[i + 1, pl.ds(j, n)]
        beside = beside + (ref[i, pl.ds(j - 1, n)] + ref[i, pl.ds(j + 1, n)])
        return center, beside + beside_z(center, step)

    left = jnp.where(gy > 0, 1.0, 0.0).astype(F32)
    right = jnp.where(gy < ny - 1, 1.0, 0.0).astype(F32)

    def sweep(depth, sizes, offset, body, width=4):
        sx, sy = sizes
        low = jnp.where(gx > 0, offset - depth, offset)
        high = jnp.where(gx < nx - 1, offset + sx + depth, offset + sx)

        def row(i, carry):
            if depth:
                body(i, offset - depth, depth, left)
            for j, n in chunks(offset, offset + sy, width):
                body(i, j, n, None)
            if depth:
                body(i, offset + sy, depth, right)
            return carry

        lax.fori_loop(low, high, row, 0)

    def scaled(value, scale):
        return value if scale is None else value * scale

    receive("x1")

    def image_x(i, carry):
        numer, denom = carry
        for j, n in chunks(H, H + NY):
            center, beside = around(x_ext, i + H, j, n)
            image = 6.0 * center - beside
            for q in range(n):
                put(i * NY + j - H + q, 48, image[q])
            numer = numer + jnp.sum(center * image, axis=0)
            denom = denom + jnp.sum(center * center, axis=0)
        return numer, denom

    zero = jnp.zeros((K, NZ), F32)
    numer, denom = lax.fori_loop(0, NX, image_x, (zero, zero))
    numer = jnp.sum(numer, axis=1, keepdims=True)
    denom = jnp.sum(denom, axis=1, keepdims=True)
    lane2 = lax.broadcasted_iota(jnp.int32, (K, NZ), 1)
    th_mine[0] = jnp.where(lane2 < 64, numer, denom)
    exchange(CORE, 0, th_mine.at[0], th_core)
    th_mine[1] = th_mine[0] + th_core[0]
    exchange(PLANE, 1, th_mine.at[1], th_plane)
    th_mine[2] = tree([th_mine[1]] + [th_plane[i] for i in range(15)])
    exchange(DEPTH, 16, th_mine.at[2], th_depth)
    total = tree([th_mine[2]] + [th_depth[i] for i in range(7)])
    theta = (total / pltpu.roll(total, 64, 1))[:, 0:1]
    theta = jnp.broadcast_to(theta, (K, NZ))

    receive("p1")

    def image_p(i, carry):
        for j, n in chunks(1, 1 + NY):
            center, beside = around(p_ext, i + 1, j, n)
            image = 6.0 * center - beside
            for q in range(n):
                put(i * NY + j - 1 + q, 64, image[q])
        return carry

    lax.fori_loop(0, NX, image_p, 0)
    receive("x4")

    def residual(i, j, n, scale):
        center, beside = around(x_ext, i, j, n)
        r_ext[i, pl.ds(j, n)] = scaled((6.0 - theta) * center - beside, scale)

    sweep(3, (NX, NY), H, residual)

    def first_sweep(i, j, n, scale):
        center, beside = around(r_ext, i, j, n)
        eb[i, pl.ds(j, n)] = scaled((12.0 * center + beside) * (1.0 / 81.0), scale)

    sweep(2, (NX, NY), H, first_sweep)

    def smoothed(source, i, j, n):
        center, beside = around(source, i, j, n)
        return center * (1.0 / 3.0) + (r_ext[i, pl.ds(j, n)] + beside) * (1.0 / 9.0)

    def second_sweep(i, j, n, scale):
        ec[i, pl.ds(j, n)] = scaled(smoothed(eb, i, j, n), scale)

    def second_row(i):
        for j, n in chunks(H, H + NY):
            second_sweep(i, j, n, None)

    sweep_rows = (H, H + NX)

    def second_inner(i, carry):
        second_sweep(i, H - 1, 1, left)
        for j, n in chunks(H, H + NY):
            second_sweep(i, j, n, None)
        second_sweep(i, H + NY, 1, right)
        return carry

    lax.fori_loop(sweep_rows[0], sweep_rows[1], second_inner, 0)
    pl.when(gx > 0)(lambda: second_row(H - 1))
    pl.when(gx < nx - 1)(lambda: second_row(H + NX))

    def restrict(ci, carry):
        for j, n in chunks(H, H + NY):
            total = None
            for half in range(2):
                i = 2 * ci + half + H
                center, beside = around(ec, i, j, n)
                rest = r_ext[i, pl.ds(j, n)] - 6.0 * center + beside
                total = rest if total is None else total + rest
            for q in range(0, n, 2):
                cube = total[q] + total[q + 1]
                low, high = cube[0:8], cube[8:16]
                low = low + pltpu.roll(low, NZ - 1, 1)
                high = high + pltpu.roll(high, 1, 1)
                crp[ci + HC, (j - H + q) // 2 + HC] = jnp.where(even[0], low, high)
        return carry

    lax.fori_loop(0, CX, restrict, 0)
    send("cr")
    send("e")

    receive("cr")

    def coarse_first(i, j, n, scale):
        center, beside = around(crp, i, j, n, 2)
        ca[i, pl.ds(j, n)] = scaled(center * (1.0 / 27.0) + beside * (1.0 / 324.0), scale)

    def coarse_next(source, target, shift):
        def body(i, j, n, scale):
            center, beside = around(source, i, j, n, 2)
            value = center * (1.0 / 3.0) + crp[i, pl.ds(j, n)] * (1.0 / 36.0) + beside * (1.0 / 9.0)
            target[i - shift, pl.ds(j - shift, n)] = scaled(value, scale)
        return body

    sweep(2, (CX, CY), HC, coarse_first)
    sweep(1, (CX, CY), HC, coarse_next(ca, cb, 0))
    sweep(0, (CX, CY), HC, coarse_next(cb, cd, HC - HD))
    send("c")
    receive("e")
    receive("c")

    def correct(ci, carry):
        for cj in range(CY + 2 * HD):
            packed = cd[ci, cj]
            low = jnp.where(even[0], packed, pltpu.roll(packed, 1, 1))
            high = jnp.where(even[0], pltpu.roll(packed, NZ - 1, 1), packed)
            both = jnp.concatenate([low, high], axis=0)
            for half in range(2):
                i = 2 * ci + half
                ea[i, pl.ds(2 * cj, 2)] = ec[i, pl.ds(2 * cj, 2)] + both[None]
        return carry

    lax.fori_loop(0, CX + 2 * HD, correct, 0)

    def third_sweep(i, j, n, scale):
        eb[i, pl.ds(j, n)] = scaled(smoothed(ea, i, j, n), scale)

    def fourth_sweep(i, j, n, scale):
        ea[i, pl.ds(j, n)] = scaled(smoothed(eb, i, j, n), scale)

    sweep(2, (NX, NY), H, third_sweep)
    sweep(1, (NX, NY), H, fourth_sweep)

    def image_w(i, carry):
        for j, n in chunks(H, H + NY):
            center, beside = around(ea, i + H, j, n)
            image = 6.0 * center - beside
            for q in range(n):
                put(i * NY + j - H + q, 32, center[q])
                put(i * NY + j - H + q, 80, image[q])
        return carry

    lax.fori_loop(0, NX, image_w, 0)

    def products(i, acc):
        for j in range(0, NY, 2):
            cell = i * NY + j
            rhs = jnp.concatenate([split[cell], split[cell + 1]], axis=1)
            lhs = jnp.concatenate([rhs[0:48], rhs[128:176]], axis=0)
            acc = acc + lax.dot_general(lhs, rhs, (((1,), (1,)), ((), ())), preferred_element_type=F32)
        return acc

    acc = lax.fori_loop(0, NX, products, jnp.zeros((96, 256), F32))
    part = (acc[0:48, 0:128] + acc[0:48, 128:256]) + (acc[48:96, 0:128] + acc[48:96, 128:256])
    ar_mine[0] = part[0:24]
    ar_mine[1] = part[24:48]
    exchange(CORE, 23, ar_mine.at[1 - core], ar_core)
    ar_mine[2] = ar_mine[core] + ar_core[0]
    exchange(PLANE, 24, ar_mine.at[2], ar_plane)
    ar_mine[3] = tree([ar_mine[2]] + [ar_plane[i] for i in range(15)])
    exchange(DEPTH, 39, ar_mine.at[3], ar_depth)
    ar_full[core] = tree([ar_mine[3]] + [ar_depth[i] for i in range(7)])
    swap = pltpu.make_async_remote_copy(
        src_ref=ar_full.at[core],
        dst_ref=ar_full.at[core],
        send_sem=red_send.at[46],
        recv_sem=red_recv.at[46],
        device_id=(gx ^ 1, gy),
        device_id_type=MESH,
    )
    swap.start()
    swap.wait_send()
    swap.wait_recv()

    both = jnp.concatenate([ar_full[0], ar_full[1]], axis=0)

    def inverse_factor(matrix, size):
        rows = lax.broadcasted_iota(jnp.int32, (size, NZ), 0)
        lanes = lax.broadcasted_iota(jnp.int32, (size, NZ), 1)
        start = jnp.where(lanes < size, matrix, jnp.where(lanes == rows + 64, 1.0, 0.0))
        tiles = [start[8 * t : 8 * t + 8] for t in range(size // 8)]
        sub = lax.broadcasted_iota(jnp.int32, (8, NZ), 0)
        for k in range(size):
            t0, s0 = k // 8, k % 8
            pivot = tiles[t0][s0 : s0 + 1]
            pivot = pivot / pivot[:, k : k + 1]
            for t in range(t0, size // 8):
                column = jnp.broadcast_to(tiles[t][:, k : k + 1], (8, NZ))
                if t == t0:
                    column = jnp.where(sub > s0, column, 0.0)
                tiles[t] = tiles[t] - column * pivot
        done = jnp.concatenate(tiles, axis=0)
        diagonal = jnp.sum(jnp.where(lanes == rows, done, 0.0), axis=1, keepdims=True)
        return pltpu.roll(done / jnp.sqrt(diagonal), 64, 1)[:, 0:size]

    def dot(a, b):
        return jnp.dot(a, b, precision=HP, preferred_element_type=F32)

    def dot_t(a, b):
        return lax.dot_general(a, b, (((1,), (1,)), ((), ())), precision=HP, preferred_element_type=F32)

    proj = pltpu.roll(both, NZ - 48, 1)[:, 0:48]
    proj = 0.5 * (proj + proj.T)
    lower_inv = inverse_factor(both, 48)
    ritz = dot_t(dot(lower_inv, proj), lower_inv)
    ritz = 0.5 * (ritz + ritz.T)
    rows = lax.broadcasted_iota(jnp.int32, (K, 48), 0)
    cols = lax.broadcasted_iota(jnp.int32, (K, 48), 1)
    filtered_t = jnp.where(rows == cols, SHIFT, 0.0) - ritz[0:K]
    square = dot_t(filtered_t, filtered_t)
    square = jnp.concatenate([square, jnp.zeros((K, NZ - K), F32)], axis=1)
    small_inv = inverse_factor(square, K)
    ncells = float(NX * NY * NZ * nx * ny)
    coef_t = dot(dot(small_inv, filtered_t), lower_inv) * (ncells**0.5)

    coef_t = jnp.concatenate([coef_t, jnp.where(cols < K, 0.0, coef_t)], axis=0)
    coef_t = jnp.concatenate([coef_t, jnp.zeros((2 * K, NZ - 48), F32)], axis=1)
    high = coef_t.astype(BF16)
    low = (coef_t - high.astype(F32)).astype(BF16)
    weights = jnp.concatenate([high, low], axis=0)
    weights = jnp.concatenate([weights, weights], axis=1)

    def combine(i, carry):
        for j in range(0, NY, 2):
            cell = i * NY + j
            rhs = jnp.concatenate([split[cell], split[cell + 1]], axis=1)
            out = jnp.dot(weights, rhs, preferred_element_type=F32)
            out = out[0:32] + out[32:64]
            for q in range(2):
                out_block[pl.ds(cell + q, K, stride=NX * NY), :] = out[0:16, 128 * q : 128 * q + 128]
                out_search[pl.ds(cell + q, K, stride=NX * NY), :] = out[16:32, 128 * q : 128 * q + 128]
        return carry

    lax.fori_loop(0, NX, combine, 0)
    save_block = pltpu.make_async_copy(out_block, block_hbm, local_sem.at[0])
    save_search = pltpu.make_async_copy(out_search, search_hbm, local_sem.at[1])
    save_block.start()
    save_search.start()
    for name in GROUPS:
        sent(name)
    save_block.wait()
    save_search.wait()


def body(eigen_block, search_dirs):
    shape = eigen_block.shape
    flat = (shape[0] * shape[1] * shape[2], shape[3])
    vmem = pltpu.VMEM
    fine = (NX + 2 * H, NY + 2 * H, K, NZ)
    rough = (CX + 2 * HC, CY + 2 * HC, K // 2, NZ)
    scratch = [
        vmem(flat, F32),
        vmem(flat, F32),
        vmem(fine, F32),
        vmem((NX + 2, NY + 2, K, NZ), F32),
        vmem(fine, F32),
        vmem(fine, F32),
        vmem(fine, F32),
        vmem(fine, F32),
        vmem(rough, F32),
        vmem(rough, F32),
        vmem(rough, F32),
        vmem((CX + 2 * HD, CY + 2 * HD, K // 2, NZ), F32),
        vmem((NX * NY, 256, NZ), BF16),
        vmem(flat, F32),
        vmem(flat, F32),
        vmem((3, K, NZ), F32),
        vmem((1, K, NZ), F32),
        vmem((15, K, NZ), F32),
        vmem((7, K, NZ), F32),
        vmem((4, 24, NZ), F32),
        vmem((1, 24, NZ), F32),
        vmem((15, 24, NZ), F32),
        vmem((7, 24, NZ), F32),
        vmem((2, 24, NZ), F32),
        pltpu.SemaphoreType.DMA((COUNT,)),
        pltpu.SemaphoreType.DMA((COUNT,)),
        pltpu.SemaphoreType.DMA((47,)),
        pltpu.SemaphoreType.DMA((47,)),
        pltpu.SemaphoreType.DMA((2,)),
    ]
    block, search = pl.pallas_call(
        kernel,
        out_shape=(jax.ShapeDtypeStruct(flat, F32), jax.ShapeDtypeStruct(flat, F32)),
        in_specs=[pl.BlockSpec(memory_space=pl.ANY)] * 2,
        out_specs=(pl.BlockSpec(memory_space=pl.ANY), pl.BlockSpec(memory_space=pl.ANY)),
        scratch_shapes=scratch,
        compiler_params=pltpu.CompilerParams(
            collective_id=0, has_side_effects=True, vmem_limit_bytes=56 * 1024 * 1024
        ),
    )(eigen_block.reshape(flat), search_dirs.reshape(flat))
    return block.reshape(shape), search.reshape(shape)


def solution(mesh):
    spec = P(None, "gx", "gy", None)
    return jax.shard_map(body, mesh=mesh, in_specs=(spec, spec), out_specs=(spec, spec), check_vma=False)
```

```python
import functools

import jax
import jax.numpy as jnp
from jax import lax
from jax.experimental import pallas as pl
from jax.experimental.pallas import tpu as pltpu
from jax.sharding import PartitionSpec as P

MESH = pl.DeviceIdType.MESH
HP = lax.Precision.HIGHEST
F32 = jnp.float32
BF16 = jnp.bfloat16

K = 16
NX, NY, NZ = 8, 16, 128
H = 4
CX, CY = NX // 2, NY // 2
HC = 4
HD = 1
SHIFT = 13.0
X, PD, IX, IP, W, IW = 0, 16, 32, 48, 64, 80

DIRS = [(-1, 0), (1, 0), (0, -1), (0, 1), (-1, -1), (-1, 1), (1, -1), (1, 1)]


def masks_of(bits):
    out = [(0, 0)]
    for bx, by in bits:
        out = out + [(x | bx, y | by) for x, y in out]
    return out[1:]


CORE = masks_of([(1, 0)])
PLANE = masks_of([(2, 0), (0, 1), (4, 0), (8, 0)])
DEPTH = masks_of([(0, 2), (0, 4), (0, 8)])


def span(step, layers, size, offset):
    if step == 0:
        return (offset, offset, size)
    first, last = layers
    count = last - first + 1
    if step < 0:
        return (offset + first - 1, offset + size + first - 1, count)
    return (offset + size - last, offset - last, count)


def transfers():
    groups = {}
    groups["x1"] = [("x", d, (1, 1), (1, 1)) for d in range(4)]
    groups["x2"] = [("x", d, (2, 2), (2, 2)) for d in range(4)] + [("x", d, (1, 1), (1, 1)) for d in range(4, 8)]
    deep = [("x", d, (3, 4), (3, 4)) for d in range(4)]
    for d in range(4, 8):
        deep += [("x", d, (1, 1), (2, 3)), ("x", d, (2, 2), (1, 2)), ("x", d, (3, 3), (1, 1))]
    groups["x4"] = deep
    groups["p1"] = [("p", d, (1, 1), (1, 1)) for d in (1, 3)]
    groups["w1"] = [("w", d, (1, 1), (1, 1)) for d in (1, 3)]
    rough = [("cr", d, (1, 4), (1, 4)) for d in range(4)]
    for d in range(4, 8):
        rough += [("cr", d, (1, 1), (1, 3)), ("cr", d, (2, 2), (1, 2)), ("cr", d, (3, 3), (1, 1))]
    groups["cr"] = rough
    sums = [("s", d, (3, 3), (3, 3)) for d in range(4)]
    for d in range(4, 8):
        sums += [("s", d, (1, 1), (2, 2)), ("s", d, (2, 2), (1, 1))]
    groups["s"] = sums
    return groups


GROUPS = transfers()
FIRST = {}
COUNT = 0
for _name in GROUPS:
    FIRST[_name] = COUNT
    COUNT += len(GROUPS[_name])

GEOMETRY = {"x": (NX, NY, H), "p": (NX, NY, 1), "w": (NX, NY, 1), "s": (NX, NY, H), "cr": (CX, CY, HC)}


def tree(parts):
    while len(parts) > 1:
        parts = [parts[i] + parts[i + 1] for i in range(0, len(parts), 2)]
    return parts[0]


def chunks(start, stop, width=4):
    return [(j, min(width, stop - j)) for j in range(start, stop, width)]


def kernel(
    x_hbm, p_hbm, block_hbm, search_hbm,
    x_nat, p_nat, x_ext, p_ext, w_ext, r_ext, ea, eb, ec, s_ext, crp, ca, cb, cd, split, out_block, out_search,
    th_mine, th_core, th_plane, th_depth, ar_mine, ar_core, ar_plane, ar_depth, ar_full,
    send_sem, recv_sem, red_send, red_recv, local_sem,
):
    gx, gy = lax.axis_index("gx"), lax.axis_index("gy")
    nx, ny = lax.axis_size("gx"), lax.axis_size("gy")
    core = lax.rem(gx, 2)
    load_x = pltpu.make_async_copy(x_hbm, x_nat, local_sem.at[0])
    load_p = pltpu.make_async_copy(p_hbm, p_nat, local_sem.at[1])
    load_x.start()
    load_p.start()

    buffers = {"x": x_ext, "p": p_ext, "s": s_ext, "cr": crp, "w": w_ext}
    lane = lax.broadcasted_iota(jnp.int32, (1, 1, NZ), 2)
    first_z, last_z, even = lane == 0, lane == NZ - 1, lane % 2 == 0

    def exists(d, sign):
        dx, dy = DIRS[d]
        tests = []
        if dx:
            tests.append(gx > 0 if dx * sign < 0 else gx < nx - 1)
        if dy:
            tests.append(gy > 0 if dy * sign < 0 else gy < ny - 1)
        return functools.reduce(jnp.logical_and, tests)

    def copy_of(name, index):
        key, d, rows, cols = GROUPS[name][index]
        dx, dy = DIRS[d]
        sx, sy, offset = GEOMETRY[key]
        rs, rd, rn = span(dx, rows, sx, offset)
        cs, cd_, cn = span(dy, cols, sy, offset)
        buf = buffers[key]
        sem = FIRST[name] + index
        return d, pltpu.make_async_remote_copy(
            src_ref=buf.at[pl.ds(rs, rn), pl.ds(cs, cn)],
            dst_ref=buf.at[pl.ds(rd, rn), pl.ds(cd_, cn)],
            send_sem=send_sem.at[sem],
            recv_sem=recv_sem.at[sem],
            device_id=(gx + dx, gy + dy),
            device_id_type=MESH,
        )

    def send(name):
        for index in range(len(GROUPS[name])):
            d, copy = copy_of(name, index)
            pl.when(exists(d, 1))(copy.start)

    def receive(name):
        for index in range(len(GROUPS[name])):
            d, copy = copy_of(name, index)
            pl.when(exists(d, -1))(copy.wait_recv)

    def sent(name):
        for index in range(len(GROUPS[name])):
            d, copy = copy_of(name, index)
            pl.when(exists(d, 1))(copy.wait_send)

    def exchange(masks, base, source, slots):
        copies = [
            pltpu.make_async_remote_copy(
                src_ref=source,
                dst_ref=slots.at[i],
                send_sem=red_send.at[base + i],
                recv_sem=red_recv.at[base + i],
                device_id=(gx ^ mx, gy ^ my),
                device_id_type=MESH,
            )
            for i, (mx, my) in enumerate(masks)
        ]
        for copy in copies:
            copy.start()

        def finish():
            for copy in copies:
                copy.wait_send()
                copy.wait_recv()

        return finish

    barrier = pltpu.get_barrier_semaphore()
    partners = CORE + PLANE + DEPTH
    for mx, my in partners:
        pl.semaphore_signal(barrier, inc=1, device_id=(gx ^ mx, gy ^ my), device_id_type=MESH)

    def clear(ref, offset, always=False):
        rows, cols = ref.shape[:2]

        def block(i, j, n, m):
            ref[pl.ds(i, n), pl.ds(j, m)] = jnp.zeros((n, m) + tuple(ref.shape[2:]), ref.dtype)

        def lines(first):
            def line(i, carry):
                block(i, 0, 1, cols)
                return carry
            lax.fori_loop(first, first + offset, line, 0)

        def columns(first):
            def line(i, carry):
                block(i, first, 1, offset)
                return carry
            lax.fori_loop(0, rows, line, 0)

        def where(test, fill, first):
            if always:
                fill(first)
            else:
                pl.when(test)(lambda: fill(first))

        where(gx == 0, lines, 0)
        where(gx == nx - 1, lines, rows - offset)
        where(gy == 0, columns, 0)
        where(gy == ny - 1, columns, cols - offset)

    clear(x_ext, H)
    clear(p_ext, 1, always=True)
    clear(w_ext, 1, always=True)
    clear(s_ext, H)
    clear(crp, HC)

    expected = 0
    for d in range(8):
        dx, dy = DIRS[d]
        there = exists(d, 1)

        @pl.when(there)
        def _():
            pl.semaphore_signal(barrier, inc=1, device_id=(gx + dx, gy + dy), device_id_type=MESH)

        expected = expected + jnp.where(there, 1, 0)


    def put(cell, row, value):
        high = value.astype(BF16)
        split[cell, pl.ds(row, K)] = high
        split[cell, pl.ds(row + 128, K)] = (value - high.astype(F32)).astype(BF16)

    load_x.wait()

    def bring_x(i, carry):
        for j in range(NY):
            value = x_nat[pl.ds(i * NY + j, K, stride=NX * NY), :]
            x_ext[i + H, j + H] = value
        return carry

    lax.fori_loop(0, NX, bring_x, 0)
    pl.semaphore_wait(barrier, expected + len(partners))
    send("x1")
    send("x2")
    load_p.wait()
    clear(r_ext, H)
    clear(ea, H)
    clear(eb, H)
    clear(ec, H)
    clear(ca, HC)
    clear(cb, HC)
    clear(cd, HD)

    def bring_p(i, carry):
        for j in range(NY):
            p_ext[i + 1, j + 1] = p_nat[pl.ds(i * NY + j, K, stride=NX * NY), :]
        return carry

    lax.fori_loop(0, NX, bring_p, 0)

    def keep(i, carry):
        for j in range(NY):
            cell = i * NY + j
            put(cell, X, x_ext[i + H, j + H])
            put(cell, PD, p_ext[i + 1, j + 1])
            split[cell, pl.ds(96, 32)] = jnp.zeros((32, NZ), BF16)
            split[cell, pl.ds(224, 32)] = jnp.zeros((32, NZ), BF16)
        return carry

    lax.fori_loop(0, NX, keep, 0)

    def beside_z(center, step):
        zero = jnp.zeros_like(center)
        if step == 1:
            down = jnp.where(first_z, zero, pltpu.roll(center, 1, 2))
            up = jnp.where(last_z, zero, pltpu.roll(center, NZ - 1, 2))
        else:
            down = jnp.where(lane < 2, zero, pltpu.roll(center, 2, 2))
            up = jnp.where(lane >= NZ - 2, zero, pltpu.roll(center, NZ - 2, 2))
        return down + up

    def around(ref, i, j, n, step=1):
        line = ref[i, pl.ds(j - 1, n + 2)]
        center = line[1 : n + 1]
        beside = ref[i - 1, pl.ds(j, n)] + ref[i + 1, pl.ds(j, n)]
        beside = beside + (line[0:n] + line[2 : n + 2])
        return center, beside + beside_z(center, step)

    left = jnp.where(gy > 0, 1.0, 0.0).astype(F32)
    right = jnp.where(gy < ny - 1, 1.0, 0.0).astype(F32)

    def sweep(depth, sizes, offset, body, width=4):
        sx, sy = sizes
        low = jnp.where(gx > 0, offset - depth, offset)
        high = jnp.where(gx < nx - 1, offset + sx + depth, offset + sx)

        def row(i, carry):
            if depth:
                body(i, offset - depth, depth, left)
            for j, n in chunks(offset, offset + sy, width):
                body(i, j, n, None)
            if depth:
                body(i, offset + sy, depth, right)
            return carry

        lax.fori_loop(low, high, row, 0)

    def scaled(value, scale):
        return value if scale is None else value * scale

    receive("x1")

    def image_x(i, carry):
        numer, denom = carry
        for j, n in chunks(H, H + NY):
            center, beside = around(x_ext, i + H, j, n)
            image = 6.0 * center - beside
            for q in range(n):
                put(i * NY + j - H + q, IX, image[q])
            numer = numer + jnp.sum(center * image, axis=0)
            denom = denom + jnp.sum(center * center, axis=0)
        return numer, denom

    zero = jnp.zeros((K, NZ), F32)
    numer, denom = lax.fori_loop(0, NX, image_x, (zero, zero))
    numer = jnp.sum(numer, axis=1, keepdims=True)
    denom = jnp.sum(denom, axis=1, keepdims=True)

    def pair(cell, row, count):
        return jnp.concatenate([split[cell, pl.ds(row, count)], split[cell + 1, pl.ds(row, count)]], axis=1)

    def product(lhs, rhs, acc):
        return acc + lax.dot_general(lhs, rhs, (((1,), (1,)), ((), ())), preferred_element_type=F32)

    def early_products(i, acc):
        for j in range(0, NY, 2):
            cell = i * NY + j
            high, low = pair(cell, X, 48), pair(cell, X + 128, 48)
            rhs = jnp.concatenate([high, low], axis=0)
            lhs = jnp.concatenate([high[0:32], low[0:32]], axis=0)
            acc = product(lhs, rhs, acc)
        return acc

    early = lax.fori_loop(0, NX, early_products, jnp.zeros((64, 96), F32))
    early = jnp.concatenate([early[0:32] + early[32:64], jnp.zeros((32, 32), F32)], axis=1)
    early = early + pltpu.roll(early, NZ - 48, 1)
    lane2 = lax.broadcasted_iota(jnp.int32, (K, NZ), 1)
    ratio = jnp.where(lane2 < 112, numer, denom)
    early = jnp.where(lane2 < 48, early[0:16], jnp.where(lane2 < 96, pltpu.roll(early[16:32], 48, 1), ratio))
    th_mine[0] = early
    exchange(CORE, 0, th_mine.at[0], th_core)()
    th_mine[1] = th_mine[0] + th_core[0]
    plane_done = exchange(PLANE, 1, th_mine.at[1], th_plane)
    send("x4")

    receive("x2")

    def power_1(i, j, n, scale):
        center, beside = around(x_ext, i, j, n)
        ea[i, pl.ds(j, n)] = scaled(center * (1.0 / 3.0) + beside * (1.0 / 9.0), scale)

    def cross_line(i):
        for j, n in chunks(H, H + NY):
            power_1(i, j, n, None)

    def cross(i, carry):
        power_1(i, H - 1, 1, left)
        cross_line(i)
        power_1(i, H + NY, 1, right)
        return carry

    lax.fori_loop(H, H + NX, cross, 0)
    pl.when(gx > 0)(lambda: cross_line(H - 1))
    pl.when(gx < nx - 1)(lambda: cross_line(H + NX))

    def sum_inner(i, j, n, scale):
        center, beside = around(ea, i, j, n)
        s_ext[i, pl.ds(j, n)] = x_ext[i, pl.ds(j, n)] + (center * (4.0 / 3.0) + beside * (1.0 / 9.0))

    sweep(0, (NX, NY), H, sum_inner)
    send("s")
    plane_done()
    th_mine[2] = tree([th_mine[1]] + [th_plane[i] for i in range(15)])
    depth_done = exchange(DEPTH, 16, th_mine.at[2], th_depth)

    receive("x4")

    def power_2(i, j, n, scale):
        center, beside = around(ea, i, j, n)
        eb[i, pl.ds(j, n)] = scaled(center * (1.0 / 3.0) + beside * (1.0 / 9.0), scale)

    def power_3(i, j, n, scale):
        center, beside = around(eb, i, j, n)
        ec[i, pl.ds(j, n)] = scaled(center * (1.0 / 3.0) + beside * (1.0 / 9.0), scale)

    sweep(3, (NX, NY), H, power_1)
    sweep(2, (NX, NY), H, power_2)
    sweep(1, (NX, NY), H, power_3)
    depth_done()
    total = tree([th_mine[2]] + [th_depth[i] for i in range(7)])
    theta = jnp.broadcast_to(total[:, 96:97] / total[:, 112:113], (K, NZ))
    shifted = 6.0 - theta

    def restrict(ci, carry):
        for j, n in chunks(H, H + NY):
            total = None
            for half in range(2):
                center, beside = around(ec, 2 * ci + half + H, j, n)
                rest = shifted * center - beside
                total = rest if total is None else total + rest
            for q in range(0, n, 2):
                cube = total[q] + total[q + 1]
                low, high = cube[0:8], cube[8:16]
                low = low + pltpu.roll(low, NZ - 1, 1)
                high = high + pltpu.roll(high, 1, 1)
                crp[ci + HC, (j - H + q) // 2 + HC] = jnp.where(even[0], low, high)
        return carry

    lax.fori_loop(0, CX, restrict, 0)
    send("cr")
    send("p1")

    def sum_outer(i, j, n):
        s_ext[i, pl.ds(j, n)] = x_ext[i, pl.ds(j, n)] + ea[i, pl.ds(j, n)] + eb[i, pl.ds(j, n)]

    def sum_sides(i, carry):
        sum_outer(i, H - 2, 2)
        sum_outer(i, H + NY, 2)
        return carry

    lax.fori_loop(H, H + NX, sum_sides, 0)
    for i in (H - 2, H - 1, H + NX, H + NX + 1):
        for j, n in chunks(H, H + NY):
            sum_outer(i, j, n)
    for i in (H - 1, H + NX):
        sum_outer(i, H - 1, 1)
        sum_outer(i, H + NY, 1)
    receive("s")

    def second_sweep(i, j, n, scale):
        center, beside = around(s_ext, i, j, n)
        ec[i, pl.ds(j, n)] = scaled((shifted * center - beside) * (1.0 / 9.0), scale)

    sweep(2, (NX, NY), H, second_sweep)

    def residual(i, j, n, scale):
        center, beside = around(x_ext, i, j, n)
        r_ext[i, pl.ds(j, n)] = scaled(shifted * center - beside, scale)

    sweep(2, (NX, NY), H, residual)

    def smoothed(source, i, j, n):
        center, beside = around(source, i, j, n)
        return center * (1.0 / 3.0) + (r_ext[i, pl.ds(j, n)] + beside) * (1.0 / 9.0)

    receive("cr")

    def coarse_first(i, j, n, scale):
        center, beside = around(crp, i, j, n, 2)
        ca[i, pl.ds(j, n)] = scaled(center * (1.0 / 27.0) + beside * (1.0 / 324.0), scale)

    def coarse_next(source, target, shift):
        def body(i, j, n, scale):
            center, beside = around(source, i, j, n, 2)
            value = center * (1.0 / 3.0) + crp[i, pl.ds(j, n)] * (1.0 / 36.0) + beside * (1.0 / 9.0)
            target[i - shift, pl.ds(j - shift, n)] = scaled(value, scale)
        return body

    sweep(3, (CX, CY), HC, coarse_first)
    sweep(2, (CX, CY), HC, coarse_next(ca, cb, 0))
    sweep(1, (CX, CY), HC, coarse_next(cb, cd, HC - HD))
    def correct(ci, carry):
        for cj in range(CY + 2 * HD):
            packed = cd[ci, cj]
            low = jnp.where(even[0], packed, pltpu.roll(packed, 1, 1))
            high = jnp.where(even[0], pltpu.roll(packed, NZ - 1, 1), packed)
            both = jnp.concatenate([low, high], axis=0)
            for half in range(2):
                i, j = 2 * (ci - HD) + half + H, 2 * (cj - HD) + H
                ea[i, pl.ds(j, 2)] = ec[i, pl.ds(j, 2)] + both[None]
        return carry

    lax.fori_loop(0, CX + 2 * HD, correct, 0)

    def third_sweep(i, j, n, scale):
        eb[i, pl.ds(j, n)] = scaled(smoothed(ea, i, j, n), scale)

    def fourth_sweep(i, j, n, scale):
        value = smoothed(eb, i, j, n)
        w_ext[i - H + 1, pl.ds(j - H + 1, n)] = value
        for q in range(n):
            put((i - H) * NY + j - H + q, W, value[q])

    sweep(1, (NX, NY), H, third_sweep)
    sweep(0, (NX, NY), H, fourth_sweep)
    send("w1")

    def half_image(ref, row):
        def double(i, carry):
            ref[i, 0] = ref[i, 0] * 2.0
            return carry

        lax.fori_loop(1, 1 + NX, double, 0)
        for j, n in chunks(1, 1 + NY):
            ref[0, pl.ds(j, n)] = ref[0, pl.ds(j, n)] * 2.0

        def image_row(i, carry):
            for j, n in chunks(1, 1 + NY):
                center, beside = around(ref, i + 1, j, n)
                image = 6.0 * center - beside
                for q in range(n):
                    put(i * NY + j - 1 + q, row, image[q])
            return carry

        lax.fori_loop(0, NX, image_row, 0)

    receive("p1")
    half_image(p_ext, IP)

    def late_products(i, acc):
        for j in range(0, NY, 2):
            cell = i * NY + j
            high, low = pair(cell, X, 80), pair(cell, X + 128, 80)
            rhs = jnp.concatenate([high[48:80], low[48:80]], axis=0)
            acc = product(jnp.concatenate([high, low], axis=0), rhs, acc)
        return acc

    late = lax.fori_loop(0, NX, late_products, jnp.zeros((160, 64), F32))
    receive("w1")
    half_image(w_ext, IW)

    def last_products(i, acc):
        for j in range(0, NY, 2):
            cell = i * NY + j
            rhs = jnp.concatenate([pair(cell, IW, 16), pair(cell, IW + 128, 16)], axis=0)
            lhs = [pair(cell, row, 16) for row in (PD, W, PD + 128, W + 128)]
            acc = product(jnp.concatenate(lhs, axis=0), rhs, acc)
        return acc

    last = lax.fori_loop(0, NX, last_products, jnp.zeros((64, 32), F32))

    def folded(value, half, width):
        value = value[0:half] + value[half : 2 * half]
        value = jnp.concatenate([value, jnp.zeros((half, NZ - 2 * width), F32)], axis=1)
        return value + pltpu.roll(value, NZ - width, 1)

    late = folded(late, 80, 32)
    last = folded(last, 32, 16)

    def moved(value, start, end):
        return pltpu.roll(value, (end - start) % NZ, 1) if start != end else value

    mixed = 0.5 * (moved(late[48:64], 16, 48) + moved(last[0:16], 0, 48))
    blocks = [
        moved(late[0:16], 16, 0),
        late[32:48],
        moved(late[16:32], 16, 32),
        mixed,
        moved(late[64:80], 16, 64),
        moved(last[16:32], 0, 80),
        moved(late[16:32], 0, 96),
    ]
    part = jnp.zeros((K, NZ), F32)
    for index, block in enumerate(blocks):
        part = jnp.where(lane2 // K == index, block, part)
    ar_mine[0] = part[0:8]
    ar_mine[1] = part[8:16]
    exchange(CORE, 23, ar_mine.at[1 - core], ar_core)()
    ar_mine[2] = ar_mine[core] + ar_core[0]
    exchange(PLANE, 24, ar_mine.at[2], ar_plane)()
    ar_mine[3] = tree([ar_mine[2]] + [ar_plane[i] for i in range(15)])
    exchange(DEPTH, 39, ar_mine.at[3], ar_depth)()
    ar_full[core] = tree([ar_mine[3]] + [ar_depth[i] for i in range(7)])
    swap = pltpu.make_async_remote_copy(
        src_ref=ar_full.at[core],
        dst_ref=ar_full.at[core],
        send_sem=red_send.at[46],
        recv_sem=red_recv.at[46],
        device_id=(gx ^ 1, gy),
        device_id_type=MESH,
    )
    swap.start()
    swap.wait_send()
    swap.wait_recv()

    both = jnp.concatenate([ar_full[0], ar_full[1]], axis=0)

    def inverse_factor(matrix, size):
        rows = lax.broadcasted_iota(jnp.int32, (size, NZ), 0)
        lanes = lax.broadcasted_iota(jnp.int32, (size, NZ), 1)
        start = jnp.where(lanes < size, matrix, jnp.where(lanes == rows + 64, 1.0, 0.0))
        tiles = [start[8 * t : 8 * t + 8] for t in range(size // 8)]
        sub = lax.broadcasted_iota(jnp.int32, (8, NZ), 0)
        for k in range(size):
            t0, s0 = k // 8, k % 8
            pivot = tiles[t0][s0 : s0 + 1]
            pivot = pivot / pivot[:, k : k + 1]
            for t in range(t0, size // 8):
                column = jnp.broadcast_to(tiles[t][:, k : k + 1], (8, NZ))
                if t == t0:
                    column = jnp.where(sub > s0, column, 0.0)
                tiles[t] = tiles[t] - column * pivot
        done = jnp.concatenate(tiles, axis=0)
        diagonal = jnp.sum(jnp.where(lanes == rows, done, 0.0), axis=1, keepdims=True)
        return pltpu.roll(done / jnp.sqrt(diagonal), 64, 1)[:, 0:size]

    def dot(a, b):
        return jnp.dot(a, b, precision=HP, preferred_element_type=F32)

    def dot_t(a, b):
        return lax.dot_general(a, b, (((1,), (1,)), ((), ())), precision=HP, preferred_element_type=F32)

    rows = lax.broadcasted_iota(jnp.int32, (48, 48), 0)
    cols = lax.broadcasted_iota(jnp.int32, (48, 48), 1)

    def upper(first, second, third):
        return jnp.concatenate([first, second, third], axis=0)[:, 0:48]

    x_rows, p_rows = total, moved(total, 48, 0)
    gram = upper(
        jnp.where(lane2 < 32, x_rows, moved(both, 0, 32)), jnp.where(lane2 < 32, p_rows, both), moved(both, 64, 32)
    )
    gram = jnp.where(jnp.logical_and(rows >= 32, cols < 32), gram.T, gram)
    proj = upper(
        jnp.where(lane2 < 32, moved(x_rows, 32, 0), moved(both, 16, 32)),
        jnp.where(lane2 < 16, moved(p_rows, 32, 0), jnp.where(lane2 < 32, moved(both, 96, 16), moved(both, 48, 32))),
        moved(both, 80, 32),
    )
    below = jnp.logical_and(rows >= 32, cols < 32)
    beside_x = jnp.logical_and(rows < 16, jnp.logical_and(cols >= 16, cols < 32))
    proj = jnp.where(jnp.logical_or(below, beside_x), proj.T, proj)
    proj = 0.5 * (proj + proj.T)
    lower_inv = inverse_factor(jnp.concatenate([gram, jnp.zeros((48, NZ - 48), F32)], axis=1), 48)
    ritz = dot_t(dot(lower_inv, proj), lower_inv)
    ritz = 0.5 * (ritz + ritz.T)
    rows = lax.broadcasted_iota(jnp.int32, (K, 48), 0)
    cols = lax.broadcasted_iota(jnp.int32, (K, 48), 1)
    filtered_t = jnp.where(rows == cols, SHIFT, 0.0) - ritz[0:K]
    square = dot_t(filtered_t, filtered_t)
    square = jnp.concatenate([square, jnp.zeros((K, NZ - K), F32)], axis=1)
    small_inv = inverse_factor(square, K)
    ncells = float(NX * NY * NZ * nx * ny)
    coef_t = dot(dot(small_inv, filtered_t), lower_inv) * (ncells**0.5)

    coef_t = jnp.concatenate([coef_t, jnp.where(cols < K, 0.0, coef_t)], axis=0)
    gap = jnp.zeros((2 * K, 32), F32)
    coef_t = jnp.concatenate([coef_t[:, 0:32], gap, coef_t[:, 32:48], gap, gap[:, 0:16]], axis=1)
    high = coef_t.astype(BF16)
    low = (coef_t - high.astype(F32)).astype(BF16)
    weights = jnp.concatenate([high, low], axis=0)
    weights = jnp.concatenate([weights, weights], axis=1)

    def combine(i, carry):
        for j in range(0, NY, 2):
            cell = i * NY + j
            rhs = jnp.concatenate([split[cell], split[cell + 1]], axis=1)
            out = jnp.dot(weights, rhs, preferred_element_type=F32)
            out = out[0:32] + out[32:64]
            for q in range(2):
                out_block[pl.ds(cell + q, K, stride=NX * NY), :] = out[0:16, 128 * q : 128 * q + 128]
                out_search[pl.ds(cell + q, K, stride=NX * NY), :] = out[16:32, 128 * q : 128 * q + 128]
        return carry

    lax.fori_loop(0, NX, combine, 0)
    save_block = pltpu.make_async_copy(out_block, block_hbm, local_sem.at[0])
    save_search = pltpu.make_async_copy(out_search, search_hbm, local_sem.at[1])
    save_block.start()
    save_search.start()
    for name in GROUPS:
        sent(name)
    save_block.wait()
    save_search.wait()


def body(eigen_block, search_dirs):
    shape = eigen_block.shape
    flat = (shape[0] * shape[1] * shape[2], shape[3])
    vmem = pltpu.VMEM
    fine = (NX + 2 * H, NY + 2 * H, K, NZ)
    rough = (CX + 2 * HC, CY + 2 * HC, K // 2, NZ)
    scratch = [
        vmem(flat, F32),
        vmem(flat, F32),
        vmem(fine, F32),
        vmem((NX + 2, NY + 2, K, NZ), F32),
        vmem((NX + 2, NY + 2, K, NZ), F32),
        vmem(fine, F32),
        vmem(fine, F32),
        vmem(fine, F32),
        vmem(fine, F32),
        vmem(fine, F32),
        vmem(rough, F32),
        vmem(rough, F32),
        vmem(rough, F32),
        vmem((CX + 2 * HD, CY + 2 * HD, K // 2, NZ), F32),
        vmem((NX * NY, 256, NZ), BF16),
        vmem(flat, F32),
        vmem(flat, F32),
        vmem((3, K, NZ), F32),
        vmem((1, K, NZ), F32),
        vmem((15, K, NZ), F32),
        vmem((7, K, NZ), F32),
        vmem((4, 8, NZ), F32),
        vmem((1, 8, NZ), F32),
        vmem((15, 8, NZ), F32),
        vmem((7, 8, NZ), F32),
        vmem((2, 8, NZ), F32),
        pltpu.SemaphoreType.DMA((COUNT,)),
        pltpu.SemaphoreType.DMA((COUNT,)),
        pltpu.SemaphoreType.DMA((47,)),
        pltpu.SemaphoreType.DMA((47,)),
        pltpu.SemaphoreType.DMA((2,)),
    ]
    block, search = pl.pallas_call(
        kernel,
        out_shape=(jax.ShapeDtypeStruct(flat, F32), jax.ShapeDtypeStruct(flat, F32)),
        in_specs=[pl.BlockSpec(memory_space=pl.ANY)] * 2,
        out_specs=(pl.BlockSpec(memory_space=pl.ANY), pl.BlockSpec(memory_space=pl.ANY)),
        scratch_shapes=scratch,
        compiler_params=pltpu.CompilerParams(
            collective_id=0, has_side_effects=True, vmem_limit_bytes=56 * 1024 * 1024
        ),
    )(eigen_block.reshape(flat), search_dirs.reshape(flat))
    return block.reshape(shape), search.reshape(shape)


def solution(mesh):
    spec = P(None, "gx", "gy", None)
    return jax.shard_map(body, mesh=mesh, in_specs=(spec, spec), out_specs=(spec, spec), check_vma=False)
```

```python
import functools

import jax
import jax.numpy as jnp
from jax import lax
from jax.experimental import pallas as pl
from jax.experimental.pallas import tpu as pltpu
from jax.sharding import PartitionSpec as P

MESH = pl.DeviceIdType.MESH
HP = lax.Precision.HIGHEST
F32 = jnp.float32
BF16 = jnp.bfloat16

K = 16
NX, NY, NZ = 8, 16, 128
H = 4
CX, CY = NX // 2, NY // 2
HC = 4
HD = 1
SHIFT = 13.0
X, PD, IX, IP, W, IW = 0, 16, 32, 48, 64, 80

DIRS = [(-1, 0), (1, 0), (0, -1), (0, 1), (-1, -1), (-1, 1), (1, -1), (1, 1)]


def masks_of(bits):
    out = [(0, 0)]
    for bx, by in bits:
        out = out + [(x | bx, y | by) for x, y in out]
    return out[1:]


CORE = masks_of([(1, 0)])
PLANE = masks_of([(2, 0), (0, 1), (4, 0), (8, 0)])
DEPTH = masks_of([(0, 2), (0, 4), (0, 8)])


def span(step, layers, size, offset):
    if step == 0:
        return (offset, offset, size)
    first, last = layers
    count = last - first + 1
    if step < 0:
        return (offset + first - 1, offset + size + first - 1, count)
    return (offset + size - last, offset - last, count)


def transfers():
    groups = {}
    groups["x1"] = [("x", d, (1, 1), (1, 1)) for d in range(4)]
    groups["x2"] = [("x", d, (2, 2), (2, 2)) for d in range(4)] + [("x", d, (1, 1), (1, 1)) for d in range(4, 8)]
    deep = [("x", d, (3, 4), (3, 4)) for d in range(4)]
    for d in range(4, 8):
        deep += [("x", d, (1, 1), (2, 3)), ("x", d, (2, 2), (1, 2)), ("x", d, (3, 3), (1, 1))]
    groups["x4"] = deep
    groups["p1"] = [("p", d, (1, 1), (1, 1)) for d in (1, 3)]
    groups["w1"] = [("w", d, (1, 1), (1, 1)) for d in (1, 3)]
    rough = [("cr", d, (1, 4), (1, 4)) for d in range(4)]
    for d in range(4, 8):
        rough += [("cr", d, (1, 1), (1, 3)), ("cr", d, (2, 2), (1, 2)), ("cr", d, (3, 3), (1, 1))]
    groups["cr"] = rough
    sums = [("s", d, (3, 3), (3, 3)) for d in range(4)]
    for d in range(4, 8):
        sums += [("s", d, (1, 1), (2, 2)), ("s", d, (2, 2), (1, 1))]
    groups["s"] = sums
    return groups


GROUPS = transfers()
FIRST = {}
COUNT = 0
for _name in GROUPS:
    FIRST[_name] = COUNT
    COUNT += len(GROUPS[_name])

GEOMETRY = {"x": (NX, NY, H), "p": (NX, NY, 1), "w": (NX, NY, 1), "s": (NX, NY, H), "cr": (CX, CY, HC)}


def tree(parts):
    while len(parts) > 1:
        parts = [parts[i] + parts[i + 1] for i in range(0, len(parts), 2)]
    return parts[0]


def chunks(start, stop, width=4):
    return [(j, min(width, stop - j)) for j in range(start, stop, width)]


def kernel(
    x_hbm, p_hbm, block_hbm, search_hbm,
    x_nat, p_nat, x_ext, p_ext, w_ext, r_ext, ea, eb, ec, s_ext, crp, ca, cb, cd, split, out_block, out_search,
    th_mine, th_core, th_plane, th_depth, ar_mine, ar_core, ar_plane, ar_depth, ar_full,
    send_sem, recv_sem, red_send, red_recv, local_sem,
):
    gx, gy = lax.axis_index("gx"), lax.axis_index("gy")
    nx, ny = lax.axis_size("gx"), lax.axis_size("gy")
    core = lax.rem(gx, 2)
    load_x = pltpu.make_async_copy(x_hbm, x_nat, local_sem.at[0])
    load_p = pltpu.make_async_copy(p_hbm, p_nat, local_sem.at[1])
    load_x.start()
    load_p.start()

    buffers = {"x": x_ext, "p": p_ext, "s": s_ext, "cr": crp, "w": w_ext}
    lane = lax.broadcasted_iota(jnp.int32, (1, 1, NZ), 2)
    first_z, last_z, even = lane == 0, lane == NZ - 1, lane % 2 == 0

    def exists(d, sign):
        dx, dy = DIRS[d]
        tests = []
        if dx:
            tests.append(gx > 0 if dx * sign < 0 else gx < nx - 1)
        if dy:
            tests.append(gy > 0 if dy * sign < 0 else gy < ny - 1)
        return functools.reduce(jnp.logical_and, tests)

    def copy_of(name, index):
        key, d, rows, cols = GROUPS[name][index]
        dx, dy = DIRS[d]
        sx, sy, offset = GEOMETRY[key]
        rs, rd, rn = span(dx, rows, sx, offset)
        cs, cd_, cn = span(dy, cols, sy, offset)
        buf = buffers[key]
        sem = FIRST[name] + index
        return d, pltpu.make_async_remote_copy(
            src_ref=buf.at[pl.ds(rs, rn), pl.ds(cs, cn)],
            dst_ref=buf.at[pl.ds(rd, rn), pl.ds(cd_, cn)],
            send_sem=send_sem.at[sem],
            recv_sem=recv_sem.at[sem],
            device_id=(gx + dx, gy + dy),
            device_id_type=MESH,
        )

    def send(name):
        for index in range(len(GROUPS[name])):
            d, copy = copy_of(name, index)
            pl.when(exists(d, 1))(copy.start)

    def receive(name):
        for index in range(len(GROUPS[name])):
            d, copy = copy_of(name, index)
            pl.when(exists(d, -1))(copy.wait_recv)

    def sent(name):
        for index in range(len(GROUPS[name])):
            d, copy = copy_of(name, index)
            pl.when(exists(d, 1))(copy.wait_send)

    def exchange(masks, base, source, slots):
        copies = [
            pltpu.make_async_remote_copy(
                src_ref=source,
                dst_ref=slots.at[i],
                send_sem=red_send.at[base + i],
                recv_sem=red_recv.at[base + i],
                device_id=(gx ^ mx, gy ^ my),
                device_id_type=MESH,
            )
            for i, (mx, my) in enumerate(masks)
        ]
        for copy in copies:
            copy.start()

        def finish():
            for copy in copies:
                copy.wait_send()
                copy.wait_recv()

        return finish

    barrier = pltpu.get_barrier_semaphore()
    partners = CORE + PLANE + DEPTH
    for mx, my in partners:
        pl.semaphore_signal(barrier, inc=1, device_id=(gx ^ mx, gy ^ my), device_id_type=MESH)

    def clear(ref, offset, always=False):
        rows, cols = ref.shape[:2]

        def block(i, j, n, m):
            ref[pl.ds(i, n), pl.ds(j, m)] = jnp.zeros((n, m) + tuple(ref.shape[2:]), ref.dtype)

        def lines(first):
            def line(i, carry):
                block(i, 0, 1, cols)
                return carry
            lax.fori_loop(first, first + offset, line, 0)

        def columns(first):
            def line(i, carry):
                block(i, first, 1, offset)
                return carry
            lax.fori_loop(0, rows, line, 0)

        def where(test, fill, first):
            if always:
                fill(first)
            else:
                pl.when(test)(lambda: fill(first))

        where(gx == 0, lines, 0)
        where(gx == nx - 1, lines, rows - offset)
        where(gy == 0, columns, 0)
        where(gy == ny - 1, columns, cols - offset)

    clear(x_ext, H)
    clear(p_ext, 1, always=True)
    clear(w_ext, 1, always=True)
    clear(s_ext, H)
    clear(crp, HC)

    expected = 0
    for d in range(8):
        dx, dy = DIRS[d]
        there = exists(d, 1)

        @pl.when(there)
        def _():
            pl.semaphore_signal(barrier, inc=1, device_id=(gx + dx, gy + dy), device_id_type=MESH)

        expected = expected + jnp.where(there, 1, 0)


    def put(cell, row, value):
        high = value.astype(BF16)
        split[cell, pl.ds(row, K)] = high
        split[cell, pl.ds(row + 128, K)] = (value - high.astype(F32)).astype(BF16)

    load_x.wait()

    def bring_x(i, carry):
        for j in range(NY):
            value = x_nat[pl.ds(i * NY + j, K, stride=NX * NY), :]
            x_ext[i + H, j + H] = value
        return carry

    lax.fori_loop(0, NX, bring_x, 0)
    pl.semaphore_wait(barrier, expected + len(partners))
    send("x1")
    send("x2")
    load_p.wait()
    clear(r_ext, H)
    clear(ea, H)
    clear(eb, H)
    clear(ec, H)
    clear(ca, HC)
    clear(cb, HC)
    clear(cd, HD)

    def bring_p(i, carry):
        for j in range(NY):
            p_ext[i + 1, j + 1] = p_nat[pl.ds(i * NY + j, K, stride=NX * NY), :]
        return carry

    lax.fori_loop(0, NX, bring_p, 0)

    def keep(i, carry):
        for j in range(NY):
            cell = i * NY + j
            put(cell, X, x_ext[i + H, j + H])
            put(cell, PD, p_ext[i + 1, j + 1])
            split[cell, pl.ds(96, 32)] = jnp.zeros((32, NZ), BF16)
            split[cell, pl.ds(224, 32)] = jnp.zeros((32, NZ), BF16)
        return carry

    lax.fori_loop(0, NX, keep, 0)

    def beside_z(center, step):
        zero = jnp.zeros_like(center)
        if step == 1:
            down = jnp.where(first_z, zero, pltpu.roll(center, 1, 2))
            up = jnp.where(last_z, zero, pltpu.roll(center, NZ - 1, 2))
        else:
            down = jnp.where(lane < 2, zero, pltpu.roll(center, 2, 2))
            up = jnp.where(lane >= NZ - 2, zero, pltpu.roll(center, NZ - 2, 2))
        return down + up

    def around(ref, i, j, n, step=1):
        line = ref[i, pl.ds(j - 1, n + 2)]
        center = line[1 : n + 1]
        beside = ref[i - 1, pl.ds(j, n)] + ref[i + 1, pl.ds(j, n)]
        beside = beside + (line[0:n] + line[2 : n + 2])
        return center, beside + beside_z(center, step)

    left = jnp.where(gy > 0, 1.0, 0.0).astype(F32)
    right = jnp.where(gy < ny - 1, 1.0, 0.0).astype(F32)

    def sweep(depth, sizes, offset, body, width=4):
        sx, sy = sizes
        low = jnp.where(gx > 0, offset - depth, offset)
        high = jnp.where(gx < nx - 1, offset + sx + depth, offset + sx)

        def row(i, carry):
            if depth:
                body(i, offset - depth, depth, left)
            for j, n in chunks(offset, offset + sy, width):
                body(i, j, n, None)
            if depth:
                body(i, offset + sy, depth, right)
            return carry

        lax.fori_loop(low, high, row, 0)

    def scaled(value, scale):
        return value if scale is None else value * scale

    receive("x1")

    def image_x(i, carry):
        numer, denom = carry
        for j, n in chunks(H, H + NY):
            center, beside = around(x_ext, i + H, j, n)
            image = 6.0 * center - beside
            for q in range(n):
                put(i * NY + j - H + q, IX, image[q])
            numer = numer + jnp.sum(center * image, axis=0)
            denom = denom + jnp.sum(center * center, axis=0)
        return numer, denom

    zero = jnp.zeros((K, NZ), F32)
    numer, denom = lax.fori_loop(0, NX, image_x, (zero, zero))
    numer = jnp.sum(numer, axis=1, keepdims=True)
    denom = jnp.sum(denom, axis=1, keepdims=True)

    def pair(cell, row, count):
        return jnp.concatenate([split[cell, pl.ds(row, count)], split[cell + 1, pl.ds(row, count)]], axis=1)

    def product(lhs, rhs, acc):
        return acc + lax.dot_general(lhs, rhs, (((1,), (1,)), ((), ())), preferred_element_type=F32)

    def early_products(i, acc):
        for j in range(0, NY, 2):
            cell = i * NY + j
            high, low = pair(cell, X, 48), pair(cell, X + 128, 48)
            rhs = jnp.concatenate([high, low], axis=0)
            lhs = jnp.concatenate([high[0:32], low[0:32]], axis=0)
            acc = product(lhs, rhs, acc)
        return acc

    early = lax.fori_loop(0, NX, early_products, jnp.zeros((64, 96), F32))
    early = jnp.concatenate([early[0:32] + early[32:64], jnp.zeros((32, 32), F32)], axis=1)
    early = early + pltpu.roll(early, NZ - 48, 1)
    lane2 = lax.broadcasted_iota(jnp.int32, (K, NZ), 1)
    ratio = jnp.where(lane2 < 112, numer, denom)
    early = jnp.where(lane2 < 48, early[0:16], jnp.where(lane2 < 96, pltpu.roll(early[16:32], 48, 1), ratio))
    th_mine[0] = early
    exchange(CORE, 0, th_mine.at[0], th_core)()
    th_mine[1] = th_mine[0] + th_core[0]
    plane_done = exchange(PLANE, 1, th_mine.at[1], th_plane)
    send("x4")

    receive("x2")

    def power_1(i, j, n, scale):
        center, beside = around(x_ext, i, j, n)
        ea[i, pl.ds(j, n)] = scaled(center * (1.0 / 3.0) + beside * (1.0 / 9.0), scale)

    def cross_line(i):
        for j, n in chunks(H, H + NY):
            power_1(i, j, n, None)

    def cross(i, carry):
        power_1(i, H - 1, 1, left)
        cross_line(i)
        power_1(i, H + NY, 1, right)
        return carry

    lax.fori_loop(H, H + NX, cross, 0)
    pl.when(gx > 0)(lambda: cross_line(H - 1))
    pl.when(gx < nx - 1)(lambda: cross_line(H + NX))

    def sum_inner(i, j, n, scale):
        center, beside = around(ea, i, j, n)
        s_ext[i, pl.ds(j, n)] = x_ext[i, pl.ds(j, n)] + (center * (4.0 / 3.0) + beside * (1.0 / 9.0))

    sweep(0, (NX, NY), H, sum_inner)
    send("s")
    plane_done()
    th_mine[2] = tree([th_mine[1]] + [th_plane[i] for i in range(15)])
    depth_done = exchange(DEPTH, 16, th_mine.at[2], th_depth)

    receive("x4")

    def power_2(i, j, n, scale):
        center, beside = around(ea, i, j, n)
        eb[i, pl.ds(j, n)] = scaled(center * (1.0 / 3.0) + beside * (1.0 / 9.0), scale)

    def power_3(i, j, n, scale):
        center, beside = around(eb, i, j, n)
        ec[i, pl.ds(j, n)] = scaled(center * (1.0 / 3.0) + beside * (1.0 / 9.0), scale)

    sweep(3, (NX, NY), H, power_1)
    sweep(2, (NX, NY), H, power_2)
    sweep(1, (NX, NY), H, power_3)
    depth_done()
    total = tree([th_mine[2]] + [th_depth[i] for i in range(7)])
    theta = jnp.broadcast_to(total[:, 96:97] / total[:, 112:113], (K, NZ))
    shifted = 6.0 - theta

    def restrict(ci, carry):
        for j, n in chunks(H, H + NY):
            total = None
            for half in range(2):
                center, beside = around(ec, 2 * ci + half + H, j, n)
                rest = shifted * center - beside
                total = rest if total is None else total + rest
            for q in range(0, n, 2):
                cube = total[q] + total[q + 1]
                low, high = cube[0:8], cube[8:16]
                low = low + pltpu.roll(low, NZ - 1, 1)
                high = high + pltpu.roll(high, 1, 1)
                crp[ci + HC, (j - H + q) // 2 + HC] = jnp.where(even[0], low, high)
        return carry

    lax.fori_loop(0, CX, restrict, 0)
    send("cr")
    send("p1")

    def sum_outer(i, j, n):
        s_ext[i, pl.ds(j, n)] = x_ext[i, pl.ds(j, n)] + ea[i, pl.ds(j, n)] + eb[i, pl.ds(j, n)]

    def sum_sides(i, carry):
        sum_outer(i, H - 2, 2)
        sum_outer(i, H + NY, 2)
        return carry

    lax.fori_loop(H, H + NX, sum_sides, 0)
    for i in (H - 2, H - 1, H + NX, H + NX + 1):
        for j, n in chunks(H, H + NY):
            sum_outer(i, j, n)
    for i in (H - 1, H + NX):
        sum_outer(i, H - 1, 1)
        sum_outer(i, H + NY, 1)
    receive("s")

    def second_sweep(i, j, n, scale):
        center, beside = around(s_ext, i, j, n)
        ec[i, pl.ds(j, n)] = scaled((shifted * center - beside) * (1.0 / 9.0), scale)

    sweep(2, (NX, NY), H, second_sweep)

    def residual(i, j, n, scale):
        center, beside = around(x_ext, i, j, n)
        r_ext[i, pl.ds(j, n)] = scaled(shifted * center - beside, scale)

    sweep(2, (NX, NY), H, residual)

    def smoothed(source, i, j, n):
        center, beside = around(source, i, j, n)
        return center * (1.0 / 3.0) + (r_ext[i, pl.ds(j, n)] + beside) * (1.0 / 9.0)

    def inverse_factor(matrix, size):
        rows = lax.broadcasted_iota(jnp.int32, (size, NZ), 0)
        lanes = lax.broadcasted_iota(jnp.int32, (size, NZ), 1)
        start = jnp.where(lanes < size, matrix, jnp.where(lanes == rows + 64, 1.0, 0.0))
        tiles = [start[8 * t : 8 * t + 8] for t in range(size // 8)]
        sub = lax.broadcasted_iota(jnp.int32, (8, NZ), 0)
        for k in range(size):
            t0, s0 = k // 8, k % 8
            pivot = tiles[t0][s0 : s0 + 1]
            pivot = pivot / pivot[:, k : k + 1]
            for t in range(t0, size // 8):
                column = jnp.broadcast_to(tiles[t][:, k : k + 1], (8, NZ))
                if t == t0:
                    column = jnp.where(sub > s0, column, 0.0)
                tiles[t] = tiles[t] - column * pivot
        done = jnp.concatenate(tiles, axis=0)
        diagonal = jnp.sum(jnp.where(lanes == rows, done, 0.0), axis=1, keepdims=True)
        return pltpu.roll(done / jnp.sqrt(diagonal), 64, 1)[:, 0:size]

    def dot(a, b):
        return jnp.dot(a, b, precision=HP, preferred_element_type=F32)

    def dot_t(a, b):
        return lax.dot_general(a, b, (((1,), (1,)), ((), ())), precision=HP, preferred_element_type=F32)

    def moved(value, start, end):
        return pltpu.roll(value, (end - start) % NZ, 1) if start != end else value

    first_inv = inverse_factor(jnp.concatenate([total, moved(total, 48, 0)], axis=0), 32)

    receive("cr")

    def coarse_first(i, j, n, scale):
        center, beside = around(crp, i, j, n, 2)
        ca[i, pl.ds(j, n)] = scaled(center * (1.0 / 27.0) + beside * (1.0 / 324.0), scale)

    def coarse_next(source, target, shift):
        def body(i, j, n, scale):
            center, beside = around(source, i, j, n, 2)
            value = center * (1.0 / 3.0) + crp[i, pl.ds(j, n)] * (1.0 / 36.0) + beside * (1.0 / 9.0)
            target[i - shift, pl.ds(j - shift, n)] = scaled(value, scale)
        return body

    sweep(3, (CX, CY), HC, coarse_first)
    sweep(2, (CX, CY), HC, coarse_next(ca, cb, 0))
    sweep(1, (CX, CY), HC, coarse_next(cb, cd, HC - HD))
    def correct(ci, carry):
        for cj in range(CY + 2 * HD):
            packed = cd[ci, cj]
            low = jnp.where(even[0], packed, pltpu.roll(packed, 1, 1))
            high = jnp.where(even[0], pltpu.roll(packed, NZ - 1, 1), packed)
            both = jnp.concatenate([low, high], axis=0)
            for half in range(2):
                i, j = 2 * (ci - HD) + half + H, 2 * (cj - HD) + H
                ea[i, pl.ds(j, 2)] = ec[i, pl.ds(j, 2)] + both[None]
        return carry

    lax.fori_loop(0, CX + 2 * HD, correct, 0)

    def third_sweep(i, j, n, scale):
        eb[i, pl.ds(j, n)] = scaled(smoothed(ea, i, j, n), scale)

    def fourth_sweep(i, j, n, scale):
        value = smoothed(eb, i, j, n)
        w_ext[i - H + 1, pl.ds(j - H + 1, n)] = value
        for q in range(n):
            put((i - H) * NY + j - H + q, W, value[q])

    sweep(1, (NX, NY), H, third_sweep)
    sweep(0, (NX, NY), H, fourth_sweep)
    send("w1")

    def half_image(ref, row):
        def double(i, carry):
            ref[i, 0] = ref[i, 0] * 2.0
            return carry

        lax.fori_loop(1, 1 + NX, double, 0)
        for j, n in chunks(1, 1 + NY):
            ref[0, pl.ds(j, n)] = ref[0, pl.ds(j, n)] * 2.0

        def image_row(i, carry):
            for j, n in chunks(1, 1 + NY):
                center, beside = around(ref, i + 1, j, n)
                image = 6.0 * center - beside
                for q in range(n):
                    put(i * NY + j - 1 + q, row, image[q])
            return carry

        lax.fori_loop(0, NX, image_row, 0)

    receive("p1")
    half_image(p_ext, IP)

    def late_products(i, acc):
        for j in range(0, NY, 2):
            cell = i * NY + j
            high, low = pair(cell, X, 80), pair(cell, X + 128, 80)
            rhs = jnp.concatenate([high[48:80], low[48:80]], axis=0)
            acc = product(jnp.concatenate([high, low], axis=0), rhs, acc)
        return acc

    late = lax.fori_loop(0, NX, late_products, jnp.zeros((160, 64), F32))
    receive("w1")
    half_image(w_ext, IW)

    def last_products(i, acc):
        for j in range(0, NY, 2):
            cell = i * NY + j
            rhs = jnp.concatenate([pair(cell, IW, 16), pair(cell, IW + 128, 16)], axis=0)
            lhs = [pair(cell, row, 16) for row in (PD, W, PD + 128, W + 128)]
            acc = product(jnp.concatenate(lhs, axis=0), rhs, acc)
        return acc

    last = lax.fori_loop(0, NX, last_products, jnp.zeros((64, 32), F32))

    def folded(value, half, width):
        value = value[0:half] + value[half : 2 * half]
        value = jnp.concatenate([value, jnp.zeros((half, NZ - 2 * width), F32)], axis=1)
        return value + pltpu.roll(value, NZ - width, 1)

    late = folded(late, 80, 32)
    last = folded(last, 32, 16)

    mixed = 0.5 * (moved(late[48:64], 16, 48) + moved(last[0:16], 0, 48))
    blocks = [
        moved(late[0:16], 16, 0),
        late[32:48],
        moved(late[16:32], 16, 32),
        mixed,
        moved(late[64:80], 16, 64),
        moved(last[16:32], 0, 80),
        moved(late[16:32], 0, 96),
    ]
    part = jnp.zeros((K, NZ), F32)
    for index, block in enumerate(blocks):
        part = jnp.where(lane2 // K == index, block, part)
    ar_mine[0] = part[0:8]
    ar_mine[1] = part[8:16]
    exchange(CORE, 23, ar_mine.at[1 - core], ar_core)()
    ar_mine[2] = ar_mine[core] + ar_core[0]
    exchange(PLANE, 24, ar_mine.at[2], ar_plane)()
    ar_mine[3] = tree([ar_mine[2]] + [ar_plane[i] for i in range(15)])
    exchange(DEPTH, 39, ar_mine.at[3], ar_depth)()
    ar_full[core] = tree([ar_mine[3]] + [ar_depth[i] for i in range(7)])
    swap = pltpu.make_async_remote_copy(
        src_ref=ar_full.at[core],
        dst_ref=ar_full.at[core],
        send_sem=red_send.at[46],
        recv_sem=red_recv.at[46],
        device_id=(gx ^ 1, gy),
        device_id_type=MESH,
    )
    swap.start()
    swap.wait_send()
    swap.wait_recv()

    both = jnp.concatenate([ar_full[0], ar_full[1]], axis=0)

    rows = lax.broadcasted_iota(jnp.int32, (48, 48), 0)
    cols = lax.broadcasted_iota(jnp.int32, (48, 48), 1)

    def upper(first, second, third):
        return jnp.concatenate([first, second, third], axis=0)[:, 0:48]

    x_rows, p_rows = total, moved(total, 48, 0)
    proj = upper(
        jnp.where(lane2 < 32, moved(x_rows, 32, 0), moved(both, 16, 32)),
        jnp.where(lane2 < 16, moved(p_rows, 32, 0), jnp.where(lane2 < 32, moved(both, 96, 16), moved(both, 48, 32))),
        moved(both, 80, 32),
    )
    below = jnp.logical_and(rows >= 32, cols < 32)
    beside_x = jnp.logical_and(rows < 16, jnp.logical_and(cols >= 16, cols < 32))
    proj = jnp.where(jnp.logical_or(below, beside_x), proj.T, proj)
    proj = 0.5 * (proj + proj.T)
    with_w = jnp.concatenate([both, moved(both, 32, 0)], axis=0)[:, 0:K]
    below_t = dot(first_inv, with_w).T
    schur = moved(both, 64, 0)[:, 0:K] - dot_t(below_t, below_t)
    last_inv = inverse_factor(jnp.concatenate([schur, jnp.zeros((K, NZ - K), F32)], axis=1), K)
    corner = dot(last_inv, dot(below_t, first_inv))
    lower_inv = jnp.concatenate(
        [
            jnp.concatenate([first_inv, jnp.zeros((32, K), F32)], axis=1),
            jnp.concatenate([-corner, last_inv], axis=1),
        ],
        axis=0,
    )
    ritz = dot_t(dot(lower_inv, proj), lower_inv)
    ritz = 0.5 * (ritz + ritz.T)
    rows = lax.broadcasted_iota(jnp.int32, (K, 48), 0)
    cols = lax.broadcasted_iota(jnp.int32, (K, 48), 1)
    filtered_t = jnp.where(rows == cols, SHIFT, 0.0) - ritz[0:K]
    square = dot_t(filtered_t, filtered_t)
    square = jnp.concatenate([square, jnp.zeros((K, NZ - K), F32)], axis=1)
    small_inv = inverse_factor(square, K)
    ncells = float(NX * NY * NZ * nx * ny)
    coef_t = dot(dot(small_inv, filtered_t), lower_inv) * (ncells**0.5)

    coef_t = jnp.concatenate([coef_t, jnp.where(cols < K, 0.0, coef_t)], axis=0)
    gap = jnp.zeros((2 * K, 32), F32)
    coef_t = jnp.concatenate([coef_t[:, 0:32], gap, coef_t[:, 32:48], gap, gap[:, 0:16]], axis=1)
    high = coef_t.astype(BF16)
    low = (coef_t - high.astype(F32)).astype(BF16)
    weights = jnp.concatenate([high, low], axis=0)
    weights = jnp.concatenate([weights, weights], axis=1)

    def combine(i, carry):
        for j in range(0, NY, 2):
            cell = i * NY + j
            rhs = jnp.concatenate([split[cell], split[cell + 1]], axis=1)
            out = jnp.dot(weights, rhs, preferred_element_type=F32)
            out = out[0:32] + out[32:64]
            for q in range(2):
                out_block[pl.ds(cell + q, K, stride=NX * NY), :] = out[0:16, 128 * q : 128 * q + 128]
                out_search[pl.ds(cell + q, K, stride=NX * NY), :] = out[16:32, 128 * q : 128 * q + 128]
        return carry

    lax.fori_loop(0, NX, combine, 0)
    save_block = pltpu.make_async_copy(out_block, block_hbm, local_sem.at[0])
    save_search = pltpu.make_async_copy(out_search, search_hbm, local_sem.at[1])
    save_block.start()
    save_search.start()
    for name in GROUPS:
        sent(name)
    save_block.wait()
    save_search.wait()


def body(eigen_block, search_dirs):
    shape = eigen_block.shape
    flat = (shape[0] * shape[1] * shape[2], shape[3])
    vmem = pltpu.VMEM
    fine = (NX + 2 * H, NY + 2 * H, K, NZ)
    rough = (CX + 2 * HC, CY + 2 * HC, K // 2, NZ)
    scratch = [
        vmem(flat, F32),
        vmem(flat, F32),
        vmem(fine, F32),
        vmem((NX + 2, NY + 2, K, NZ), F32),
        vmem((NX + 2, NY + 2, K, NZ), F32),
        vmem(fine, F32),
        vmem(fine, F32),
        vmem(fine, F32),
        vmem(fine, F32),
        vmem(fine, F32),
        vmem(rough, F32),
        vmem(rough, F32),
        vmem(rough, F32),
        vmem((CX + 2 * HD, CY + 2 * HD, K // 2, NZ), F32),
        vmem((NX * NY, 256, NZ), BF16),
        vmem(flat, F32),
        vmem(flat, F32),
        vmem((3, K, NZ), F32),
        vmem((1, K, NZ), F32),
        vmem((15, K, NZ), F32),
        vmem((7, K, NZ), F32),
        vmem((4, 8, NZ), F32),
        vmem((1, 8, NZ), F32),
        vmem((15, 8, NZ), F32),
        vmem((7, 8, NZ), F32),
        vmem((2, 8, NZ), F32),
        pltpu.SemaphoreType.DMA((COUNT,)),
        pltpu.SemaphoreType.DMA((COUNT,)),
        pltpu.SemaphoreType.DMA((47,)),
        pltpu.SemaphoreType.DMA((47,)),
        pltpu.SemaphoreType.DMA((2,)),
    ]
    block, search = pl.pallas_call(
        kernel,
        out_shape=(jax.ShapeDtypeStruct(flat, F32), jax.ShapeDtypeStruct(flat, F32)),
        in_specs=[pl.BlockSpec(memory_space=pl.ANY)] * 2,
        out_specs=(pl.BlockSpec(memory_space=pl.ANY), pl.BlockSpec(memory_space=pl.ANY)),
        scratch_shapes=scratch,
        compiler_params=pltpu.CompilerParams(
            collective_id=0, has_side_effects=True, vmem_limit_bytes=56 * 1024 * 1024
        ),
    )(eigen_block.reshape(flat), search_dirs.reshape(flat))
    return block.reshape(shape), search.reshape(shape)


def solution(mesh):
    spec = P(None, "gx", "gy", None)
    return jax.shard_map(body, mesh=mesh, in_specs=(spec, spec), out_specs=(spec, spec), check_vma=False)
```

```python
import functools

import jax
import jax.numpy as jnp
from jax import lax
from jax.experimental import pallas as pl
from jax.experimental.pallas import tpu as pltpu
from jax.sharding import PartitionSpec as P

MESH = pl.DeviceIdType.MESH
HP = lax.Precision.HIGHEST
F32 = jnp.float32
BF16 = jnp.bfloat16

K = 16
NX, NY, NZ = 8, 16, 128
H = 4
CX, CY = NX // 2, NY // 2
HC = 4
HD = 1
SHIFT = 13.0
X, PD, IX, IP, W, IW = 0, 16, 32, 48, 64, 80

DIRS = [(-1, 0), (1, 0), (0, -1), (0, 1), (-1, -1), (-1, 1), (1, -1), (1, 1)]


def masks_of(bits):
    out = [(0, 0)]
    for bx, by in bits:
        out = out + [(x | bx, y | by) for x, y in out]
    return out[1:]


CORE = masks_of([(1, 0)])
PLANE = masks_of([(2, 0), (0, 1), (4, 0), (8, 0)])
DEPTH = masks_of([(0, 2), (0, 4), (0, 8)])


def span(step, layers, size, offset):
    if step == 0:
        return (offset, offset, size)
    first, last = layers
    count = last - first + 1
    if step < 0:
        return (offset + first - 1, offset + size + first - 1, count)
    return (offset + size - last, offset - last, count)


def transfers():
    groups = {}
    groups["x1"] = [("x", d, (1, 1), (1, 1)) for d in range(4)]
    groups["x2"] = [("x", d, (2, 2), (2, 2)) for d in range(4)] + [("x", d, (1, 1), (1, 1)) for d in range(4, 8)]
    groups["x3"] = [("x", d, (3, 3), (3, 3)) for d in range(4)]
    deep = [("x", d, (4, 4), (4, 4)) for d in range(4)]
    for d in range(4, 8):
        deep += [("x", d, (1, 1), (2, 3)), ("x", d, (2, 2), (1, 2)), ("x", d, (3, 3), (1, 1))]
    groups["x4"] = deep
    groups["p1"] = [("p", d, (1, 1), (1, 1)) for d in (1, 3)]
    groups["w1"] = [("w", d, (1, 1), (1, 1)) for d in (1, 3)]
    rough = [("cr", d, (1, 4), (1, 4)) for d in range(4)]
    for d in range(4, 8):
        rough += [("cr", d, (1, 1), (1, 3)), ("cr", d, (2, 2), (1, 2)), ("cr", d, (3, 3), (1, 1))]
    groups["cr"] = rough
    sums = [("s", d, (3, 3), (3, 3)) for d in range(4)]
    for d in range(4, 8):
        sums += [("s", d, (1, 1), (2, 2)), ("s", d, (2, 2), (1, 1))]
    groups["s"] = sums
    return groups


GROUPS = transfers()
FIRST = {}
COUNT = 0
for _name in GROUPS:
    FIRST[_name] = COUNT
    COUNT += len(GROUPS[_name])

GEOMETRY = {"x": (NX, NY, H), "p": (NX, NY, 1), "w": (NX, NY, 1), "s": (NX, NY, H), "cr": (CX, CY, HC)}


def tree(parts):
    while len(parts) > 1:
        parts = [parts[i] + parts[i + 1] for i in range(0, len(parts), 2)]
    return parts[0]


def chunks(start, stop, width=4):
    return [(j, min(width, stop - j)) for j in range(start, stop, width)]


def kernel(
    x_hbm, p_hbm, block_hbm, search_hbm,
    x_nat, p_nat, x_ext, p_ext, w_ext, r_ext, ea, eb, ec, s_ext, crp, ca, cb, cd, split, out_block, out_search,
    th_mine, th_core, th_plane, th_depth, ar_mine, ar_core, ar_plane, ar_depth, ar_full,
    send_sem, recv_sem, red_send, red_recv, local_sem,
):
    gx, gy = lax.axis_index("gx"), lax.axis_index("gy")
    nx, ny = lax.axis_size("gx"), lax.axis_size("gy")
    core = lax.rem(gx, 2)
    load_x = pltpu.make_async_copy(x_hbm, x_nat, local_sem.at[0])
    load_p = pltpu.make_async_copy(p_hbm, p_nat, local_sem.at[1])
    load_x.start()
    load_p.start()

    buffers = {"x": x_ext, "p": p_ext, "s": s_ext, "cr": crp, "w": w_ext}
    lane = lax.broadcasted_iota(jnp.int32, (1, 1, NZ), 2)
    first_z, last_z, even = lane == 0, lane == NZ - 1, lane % 2 == 0

    def exists(d, sign):
        dx, dy = DIRS[d]
        tests = []
        if dx:
            tests.append(gx > 0 if dx * sign < 0 else gx < nx - 1)
        if dy:
            tests.append(gy > 0 if dy * sign < 0 else gy < ny - 1)
        return functools.reduce(jnp.logical_and, tests)

    def copy_of(name, index):
        key, d, rows, cols = GROUPS[name][index]
        dx, dy = DIRS[d]
        sx, sy, offset = GEOMETRY[key]
        rs, rd, rn = span(dx, rows, sx, offset)
        cs, cd_, cn = span(dy, cols, sy, offset)
        buf = buffers[key]
        sem = FIRST[name] + index
        return d, pltpu.make_async_remote_copy(
            src_ref=buf.at[pl.ds(rs, rn), pl.ds(cs, cn)],
            dst_ref=buf.at[pl.ds(rd, rn), pl.ds(cd_, cn)],
            send_sem=send_sem.at[sem],
            recv_sem=recv_sem.at[sem],
            device_id=(gx + dx, gy + dy),
            device_id_type=MESH,
        )

    def send(name):
        for index in range(len(GROUPS[name])):
            d, copy = copy_of(name, index)
            pl.when(exists(d, 1))(copy.start)

    def receive(name):
        for index in range(len(GROUPS[name])):
            d, copy = copy_of(name, index)
            pl.when(exists(d, -1))(copy.wait_recv)

    def sent(name):
        for index in range(len(GROUPS[name])):
            d, copy = copy_of(name, index)
            pl.when(exists(d, 1))(copy.wait_send)

    def exchange(masks, base, source, slots):
        copies = [
            pltpu.make_async_remote_copy(
                src_ref=source,
                dst_ref=slots.at[i],
                send_sem=red_send.at[base + i],
                recv_sem=red_recv.at[base + i],
                device_id=(gx ^ mx, gy ^ my),
                device_id_type=MESH,
            )
            for i, (mx, my) in enumerate(masks)
        ]
        for copy in copies:
            copy.start()

        def finish():
            for copy in copies:
                copy.wait_send()
                copy.wait_recv()

        return finish

    barrier = pltpu.get_barrier_semaphore()
    partners = CORE + PLANE + DEPTH
    for mx, my in partners:
        pl.semaphore_signal(barrier, inc=1, device_id=(gx ^ mx, gy ^ my), device_id_type=MESH)

    def clear(ref, offset, always=False):
        rows, cols = ref.shape[:2]

        def block(i, j, n, m):
            ref[pl.ds(i, n), pl.ds(j, m)] = jnp.zeros((n, m) + tuple(ref.shape[2:]), ref.dtype)

        def lines(first):
            def line(i, carry):
                block(i, 0, 1, cols)
                return carry
            lax.fori_loop(first, first + offset, line, 0)

        def columns(first):
            def line(i, carry):
                block(i, first, 1, offset)
                return carry
            lax.fori_loop(0, rows, line, 0)

        def where(test, fill, first):
            if always:
                fill(first)
            else:
                pl.when(test)(lambda: fill(first))

        where(gx == 0, lines, 0)
        where(gx == nx - 1, lines, rows - offset)
        where(gy == 0, columns, 0)
        where(gy == ny - 1, columns, cols - offset)

    clear(x_ext, H)
    clear(p_ext, 1, always=True)
    clear(w_ext, 1, always=True)
    clear(s_ext, H)
    clear(crp, HC)

    expected = 0
    for d in range(8):
        dx, dy = DIRS[d]
        there = exists(d, 1)

        @pl.when(there)
        def _():
            pl.semaphore_signal(barrier, inc=1, device_id=(gx + dx, gy + dy), device_id_type=MESH)

        expected = expected + jnp.where(there, 1, 0)


    def put(cell, row, value):
        high = value.astype(BF16)
        split[cell, pl.ds(row, K)] = high
        split[cell, pl.ds(row + 128, K)] = (value - high.astype(F32)).astype(BF16)

    load_x.wait()

    def bring_x(i, carry):
        for j in range(NY):
            value = x_nat[pl.ds(i * NY + j, K, stride=NX * NY), :]
            x_ext[i + H, j + H] = value
        return carry

    lax.fori_loop(0, NX, bring_x, 0)
    pl.semaphore_wait(barrier, expected + len(partners))
    send("x1")
    send("x2")
    send("x3")
    load_p.wait()
    clear(r_ext, H)
    clear(ea, H)
    clear(eb, H)
    clear(ec, H)
    clear(ca, HC)
    clear(cb, HC)
    clear(cd, HD)

    def bring_p(i, carry):
        for j in range(NY):
            p_ext[i + 1, j + 1] = p_nat[pl.ds(i * NY + j, K, stride=NX * NY), :]
        return carry

    lax.fori_loop(0, NX, bring_p, 0)

    def keep(i, carry):
        for j in range(NY):
            cell = i * NY + j
            put(cell, X, x_ext[i + H, j + H])
            put(cell, PD, p_ext[i + 1, j + 1])
            split[cell, pl.ds(96, 32)] = jnp.zeros((32, NZ), BF16)
            split[cell, pl.ds(224, 32)] = jnp.zeros((32, NZ), BF16)
        return carry

    lax.fori_loop(0, NX, keep, 0)

    def beside_z(center, step):
        zero = jnp.zeros_like(center)
        if step == 1:
            down = jnp.where(first_z, zero, pltpu.roll(center, 1, 2))
            up = jnp.where(last_z, zero, pltpu.roll(center, NZ - 1, 2))
        else:
            down = jnp.where(lane < 2, zero, pltpu.roll(center, 2, 2))
            up = jnp.where(lane >= NZ - 2, zero, pltpu.roll(center, NZ - 2, 2))
        return down + up

    def around(ref, i, j, n, step=1):
        line = ref[i, pl.ds(j - 1, n + 2)]
        center = line[1 : n + 1]
        beside = ref[i - 1, pl.ds(j, n)] + ref[i + 1, pl.ds(j, n)]
        beside = beside + (line[0:n] + line[2 : n + 2])
        return center, beside + beside_z(center, step)

    left = jnp.where(gy > 0, 1.0, 0.0).astype(F32)
    right = jnp.where(gy < ny - 1, 1.0, 0.0).astype(F32)

    def sweep(depth, sizes, offset, body, width=4):
        sx, sy = sizes
        low = jnp.where(gx > 0, offset - depth, offset)
        high = jnp.where(gx < nx - 1, offset + sx + depth, offset + sx)

        def row(i, carry):
            if depth:
                body(i, offset - depth, depth, left)
            for j, n in chunks(offset, offset + sy, width):
                body(i, j, n, None)
            if depth:
                body(i, offset + sy, depth, right)
            return carry

        lax.fori_loop(low, high, row, 0)

    def scaled(value, scale):
        return value if scale is None else value * scale

    receive("x1")

    def image_x(i, carry):
        numer, denom = carry
        for j, n in chunks(H, H + NY):
            center, beside = around(x_ext, i + H, j, n)
            image = 6.0 * center - beside
            for q in range(n):
                put(i * NY + j - H + q, IX, image[q])
            numer = numer + jnp.sum(center * image, axis=0)
            denom = denom + jnp.sum(center * center, axis=0)
        return numer, denom

    zero = jnp.zeros((K, NZ), F32)
    numer, denom = lax.fori_loop(0, NX, image_x, (zero, zero))
    numer = jnp.sum(numer, axis=1, keepdims=True)
    denom = jnp.sum(denom, axis=1, keepdims=True)

    def pair(cell, row, count):
        return jnp.concatenate([split[cell, pl.ds(row, count)], split[cell + 1, pl.ds(row, count)]], axis=1)

    def product(lhs, rhs, acc):
        return acc + lax.dot_general(lhs, rhs, (((1,), (1,)), ((), ())), preferred_element_type=F32)

    def early_products(i, acc):
        for j in range(0, NY, 2):
            cell = i * NY + j
            high, low = pair(cell, X, 48), pair(cell, X + 128, 48)
            rhs = jnp.concatenate([high, low], axis=0)
            lhs = jnp.concatenate([high[0:32], low[0:32]], axis=0)
            acc = product(lhs, rhs, acc)
        return acc

    early = lax.fori_loop(0, NX, early_products, jnp.zeros((64, 96), F32))
    early = jnp.concatenate([early[0:32] + early[32:64], jnp.zeros((32, 32), F32)], axis=1)
    early = early + pltpu.roll(early, NZ - 48, 1)
    lane2 = lax.broadcasted_iota(jnp.int32, (K, NZ), 1)
    ratio = jnp.where(lane2 < 112, numer, denom)
    early = jnp.where(lane2 < 48, early[0:16], jnp.where(lane2 < 96, pltpu.roll(early[16:32], 48, 1), ratio))
    th_mine[0] = early
    exchange(CORE, 0, th_mine.at[0], th_core)()
    th_mine[1] = th_mine[0] + th_core[0]
    plane_done = exchange(PLANE, 1, th_mine.at[1], th_plane)
    send("x4")

    receive("x2")

    def power_1(i, j, n, scale):
        center, beside = around(x_ext, i, j, n)
        ea[i, pl.ds(j, n)] = scaled(center * (1.0 / 3.0) + beside * (1.0 / 9.0), scale)

    def cross_line(i):
        for j, n in chunks(H, H + NY):
            power_1(i, j, n, None)

    def cross(i, carry):
        power_1(i, H - 1, 1, left)
        cross_line(i)
        power_1(i, H + NY, 1, right)
        return carry

    lax.fori_loop(H, H + NX, cross, 0)
    pl.when(gx > 0)(lambda: cross_line(H - 1))
    pl.when(gx < nx - 1)(lambda: cross_line(H + NX))

    def sum_inner(i, j, n, scale):
        center, beside = around(ea, i, j, n)
        s_ext[i, pl.ds(j, n)] = x_ext[i, pl.ds(j, n)] + (center * (4.0 / 3.0) + beside * (1.0 / 9.0))

    sweep(0, (NX, NY), H, sum_inner)
    send("s")
    plane_done()
    th_mine[2] = tree([th_mine[1]] + [th_plane[i] for i in range(15)])
    depth_done = exchange(DEPTH, 16, th_mine.at[2], th_depth)

    receive("x3")
    receive("x4")

    def power_2(i, j, n, scale):
        center, beside = around(ea, i, j, n)
        eb[i, pl.ds(j, n)] = scaled(center * (1.0 / 3.0) + beside * (1.0 / 9.0), scale)

    def power_3(i, j, n, scale):
        center, beside = around(eb, i, j, n)
        ec[i, pl.ds(j, n)] = scaled(center * (1.0 / 3.0) + beside * (1.0 / 9.0), scale)

    sweep(3, (NX, NY), H, power_1)
    sweep(2, (NX, NY), H, power_2)
    sweep(1, (NX, NY), H, power_3)
    depth_done()
    total = tree([th_mine[2]] + [th_depth[i] for i in range(7)])
    theta = jnp.broadcast_to(total[:, 96:97] / total[:, 112:113], (K, NZ))
    shifted = 6.0 - theta

    def restrict(ci, carry):
        for j, n in chunks(H, H + NY):
            total = None
            for half in range(2):
                center, beside = around(ec, 2 * ci + half + H, j, n)
                rest = shifted * center - beside
                total = rest if total is None else total + rest
            for q in range(0, n, 2):
                cube = total[q] + total[q + 1]
                low, high = cube[0:8], cube[8:16]
                low = low + pltpu.roll(low, NZ - 1, 1)
                high = high + pltpu.roll(high, 1, 1)
                crp[ci + HC, (j - H + q) // 2 + HC] = jnp.where(even[0], low, high)
        return carry

    lax.fori_loop(0, CX, restrict, 0)
    send("cr")
    send("p1")

    def sum_outer(i, j, n):
        s_ext[i, pl.ds(j, n)] = x_ext[i, pl.ds(j, n)] + ea[i, pl.ds(j, n)] + eb[i, pl.ds(j, n)]

    def sum_sides(i, carry):
        sum_outer(i, H - 2, 2)
        sum_outer(i, H + NY, 2)
        return carry

    lax.fori_loop(H, H + NX, sum_sides, 0)
    for i in (H - 2, H - 1, H + NX, H + NX + 1):
        for j, n in chunks(H, H + NY):
            sum_outer(i, j, n)
    for i in (H - 1, H + NX):
        sum_outer(i, H - 1, 1)
        sum_outer(i, H + NY, 1)
    receive("s")

    def second_sweep(i, j, n, scale):
        center, beside = around(s_ext, i, j, n)
        ec[i, pl.ds(j, n)] = scaled((shifted * center - beside) * (1.0 / 9.0), scale)

    sweep(2, (NX, NY), H, second_sweep)

    def residual(i, j, n, scale):
        center, beside = around(x_ext, i, j, n)
        r_ext[i, pl.ds(j, n)] = scaled(shifted * center - beside, scale)

    sweep(2, (NX, NY), H, residual)

    def smoothed(source, i, j, n):
        center, beside = around(source, i, j, n)
        return center * (1.0 / 3.0) + (r_ext[i, pl.ds(j, n)] + beside) * (1.0 / 9.0)

    def inverse_factor(matrix, size):
        rows = lax.broadcasted_iota(jnp.int32, (size, NZ), 0)
        lanes = lax.broadcasted_iota(jnp.int32, (size, NZ), 1)
        start = jnp.where(lanes < size, matrix, jnp.where(lanes == rows + 64, 1.0, 0.0))
        tiles = [start[8 * t : 8 * t + 8] for t in range(size // 8)]
        sub = lax.broadcasted_iota(jnp.int32, (8, NZ), 0)
        for k in range(size):
            t0, s0 = k // 8, k % 8
            pivot = tiles[t0][s0 : s0 + 1]
            pivot = pivot / pivot[:, k : k + 1]
            for t in range(t0, size // 8):
                column = jnp.broadcast_to(tiles[t][:, k : k + 1], (8, NZ))
                if t == t0:
                    column = jnp.where(sub > s0, column, 0.0)
                tiles[t] = tiles[t] - column * pivot
        done = jnp.concatenate(tiles, axis=0)
        diagonal = jnp.sum(jnp.where(lanes == rows, done, 0.0), axis=1, keepdims=True)
        return pltpu.roll(done / jnp.sqrt(diagonal), 64, 1)[:, 0:size]

    def dot(a, b):
        return jnp.dot(a, b, precision=HP, preferred_element_type=F32)

    def dot_t(a, b):
        return lax.dot_general(a, b, (((1,), (1,)), ((), ())), precision=HP, preferred_element_type=F32)

    def moved(value, start, end):
        return pltpu.roll(value, (end - start) % NZ, 1) if start != end else value

    first_inv = inverse_factor(jnp.concatenate([total, moved(total, 48, 0)], axis=0), 32)

    receive("cr")

    def coarse_first(i, j, n, scale):
        center, beside = around(crp, i, j, n, 2)
        ca[i, pl.ds(j, n)] = scaled(center * (1.0 / 27.0) + beside * (1.0 / 324.0), scale)

    def coarse_next(source, target, shift):
        def body(i, j, n, scale):
            center, beside = around(source, i, j, n, 2)
            value = center * (1.0 / 3.0) + crp[i, pl.ds(j, n)] * (1.0 / 36.0) + beside * (1.0 / 9.0)
            target[i - shift, pl.ds(j - shift, n)] = scaled(value, scale)
        return body

    sweep(3, (CX, CY), HC, coarse_first)
    sweep(2, (CX, CY), HC, coarse_next(ca, cb, 0))
    sweep(1, (CX, CY), HC, coarse_next(cb, cd, HC - HD))
    def correct(ci, carry):
        for cj in range(CY + 2 * HD):
            packed = cd[ci, cj]
            low = jnp.where(even[0], packed, pltpu.roll(packed, 1, 1))
            high = jnp.where(even[0], pltpu.roll(packed, NZ - 1, 1), packed)
            both = jnp.concatenate([low, high], axis=0)
            for half in range(2):
                i, j = 2 * (ci - HD) + half + H, 2 * (cj - HD) + H
                ea[i, pl.ds(j, 2)] = ec[i, pl.ds(j, 2)] + both[None]
        return carry

    lax.fori_loop(0, CX + 2 * HD, correct, 0)

    def third_sweep(i, j, n, scale):
        eb[i, pl.ds(j, n)] = scaled(smoothed(ea, i, j, n), scale)

    def fourth_sweep(i, j, n, scale):
        value = smoothed(eb, i, j, n)
        w_ext[i - H + 1, pl.ds(j - H + 1, n)] = value
        for q in range(n):
            put((i - H) * NY + j - H + q, W, value[q])

    sweep(1, (NX, NY), H, third_sweep)
    sweep(0, (NX, NY), H, fourth_sweep)
    send("w1")

    def half_image(ref, row):
        def double(i, carry):
            ref[i, 0] = ref[i, 0] * 2.0
            return carry

        lax.fori_loop(1, 1 + NX, double, 0)
        for j, n in chunks(1, 1 + NY):
            ref[0, pl.ds(j, n)] = ref[0, pl.ds(j, n)] * 2.0

        def image_row(i, carry):
            for j, n in chunks(1, 1 + NY):
                center, beside = around(ref, i + 1, j, n)
                image = 6.0 * center - beside
                for q in range(n):
                    put(i * NY + j - 1 + q, row, image[q])
            return carry

        lax.fori_loop(0, NX, image_row, 0)

    receive("p1")
    half_image(p_ext, IP)

    def late_products(i, acc):
        for j in range(0, NY, 2):
            cell = i * NY + j
            high, low = pair(cell, X, 80), pair(cell, X + 128, 80)
            rhs = jnp.concatenate([high[48:80], low[48:80]], axis=0)
            acc = product(jnp.concatenate([high, low], axis=0), rhs, acc)
        return acc

    late = lax.fori_loop(0, NX, late_products, jnp.zeros((160, 64), F32))
    receive("w1")
    half_image(w_ext, IW)

    def last_products(i, acc):
        for j in range(0, NY, 2):
            cell = i * NY + j
            rhs = jnp.concatenate([pair(cell, IW, 16), pair(cell, IW + 128, 16)], axis=0)
            lhs = [pair(cell, row, 16) for row in (PD, W, PD + 128, W + 128)]
            acc = product(jnp.concatenate(lhs, axis=0), rhs, acc)
        return acc

    last = lax.fori_loop(0, NX, last_products, jnp.zeros((64, 32), F32))

    def folded(value, half, width):
        value = value[0:half] + value[half : 2 * half]
        value = jnp.concatenate([value, jnp.zeros((half, NZ - 2 * width), F32)], axis=1)
        return value + pltpu.roll(value, NZ - width, 1)

    late = folded(late, 80, 32)
    last = folded(last, 32, 16)

    mixed = 0.5 * (moved(late[48:64], 16, 48) + moved(last[0:16], 0, 48))
    blocks = [
        moved(late[0:16], 16, 0),
        late[32:48],
        moved(late[16:32], 16, 32),
        mixed,
        moved(late[64:80], 16, 64),
        moved(last[16:32], 0, 80),
        moved(late[16:32], 0, 96),
    ]
    part = jnp.zeros((K, NZ), F32)
    for index, block in enumerate(blocks):
        part = jnp.where(lane2 // K == index, block, part)
    ar_mine[0] = part[0:8]
    ar_mine[1] = part[8:16]
    exchange(CORE, 23, ar_mine.at[1 - core], ar_core)()
    ar_mine[2] = ar_mine[core] + ar_core[0]
    exchange(PLANE, 24, ar_mine.at[2], ar_plane)()
    ar_mine[3] = tree([ar_mine[2]] + [ar_plane[i] for i in range(15)])
    exchange(DEPTH, 39, ar_mine.at[3], ar_depth)()
    ar_full[core] = tree([ar_mine[3]] + [ar_depth[i] for i in range(7)])
    swap = pltpu.make_async_remote_copy(
        src_ref=ar_full.at[core],
        dst_ref=ar_full.at[core],
        send_sem=red_send.at[46],
        recv_sem=red_recv.at[46],
        device_id=(gx ^ 1, gy),
        device_id_type=MESH,
    )
    swap.start()
    swap.wait_send()
    swap.wait_recv()

    both = jnp.concatenate([ar_full[0], ar_full[1]], axis=0)

    rows = lax.broadcasted_iota(jnp.int32, (48, 48), 0)
    cols = lax.broadcasted_iota(jnp.int32, (48, 48), 1)

    def upper(first, second, third):
        return jnp.concatenate([first, second, third], axis=0)[:, 0:48]

    x_rows, p_rows = total, moved(total, 48, 0)
    proj = upper(
        jnp.where(lane2 < 32, moved(x_rows, 32, 0), moved(both, 16, 32)),
        jnp.where(lane2 < 16, moved(p_rows, 32, 0), jnp.where(lane2 < 32, moved(both, 96, 16), moved(both, 48, 32))),
        moved(both, 80, 32),
    )
    below = jnp.logical_and(rows >= 32, cols < 32)
    beside_x = jnp.logical_and(rows < 16, jnp.logical_and(cols >= 16, cols < 32))
    proj = jnp.where(jnp.logical_or(below, beside_x), proj.T, proj)
    proj = 0.5 * (proj + proj.T)
    with_w = jnp.concatenate([both, moved(both, 32, 0)], axis=0)[:, 0:K]
    below_t = dot(first_inv, with_w).T
    schur = moved(both, 64, 0)[:, 0:K] - dot_t(below_t, below_t)
    last_inv = inverse_factor(jnp.concatenate([schur, jnp.zeros((K, NZ - K), F32)], axis=1), K)
    corner = dot(last_inv, dot(below_t, first_inv))
    lower_inv = jnp.concatenate(
        [
            jnp.concatenate([first_inv, jnp.zeros((32, K), F32)], axis=1),
            jnp.concatenate([-corner, last_inv], axis=1),
        ],
        axis=0,
    )
    ritz = dot_t(dot(lower_inv, proj), lower_inv)
    ritz = 0.5 * (ritz + ritz.T)
    rows = lax.broadcasted_iota(jnp.int32, (K, 48), 0)
    cols = lax.broadcasted_iota(jnp.int32, (K, 48), 1)
    filtered_t = jnp.where(rows == cols, SHIFT, 0.0) - ritz[0:K]
    square = dot_t(filtered_t, filtered_t)
    square = jnp.concatenate([square, jnp.zeros((K, NZ - K), F32)], axis=1)
    small_inv = inverse_factor(square, K)
    ncells = float(NX * NY * NZ * nx * ny)
    coef_t = dot(dot(small_inv, filtered_t), lower_inv) * (ncells**0.5)

    coef_t = jnp.concatenate([coef_t, jnp.where(cols < K, 0.0, coef_t)], axis=0)
    gap = jnp.zeros((2 * K, 32), F32)
    coef_t = jnp.concatenate([coef_t[:, 0:32], gap, coef_t[:, 32:48], gap, gap[:, 0:16]], axis=1)
    high = coef_t.astype(BF16)
    low = (coef_t - high.astype(F32)).astype(BF16)
    weights = jnp.concatenate([high, low], axis=0)
    weights = jnp.concatenate([weights, weights], axis=1)

    def combine(i, carry):
        for j in range(0, NY, 2):
            cell = i * NY + j
            rhs = jnp.concatenate([split[cell], split[cell + 1]], axis=1)
            out = jnp.dot(weights, rhs, preferred_element_type=F32)
            out = out[0:32] + out[32:64]
            for q in range(2):
                out_block[pl.ds(cell + q, K, stride=NX * NY), :] = out[0:16, 128 * q : 128 * q + 128]
                out_search[pl.ds(cell + q, K, stride=NX * NY), :] = out[16:32, 128 * q : 128 * q + 128]
        return carry

    lax.fori_loop(0, NX, combine, 0)
    save_block = pltpu.make_async_copy(out_block, block_hbm, local_sem.at[0])
    save_search = pltpu.make_async_copy(out_search, search_hbm, local_sem.at[1])
    save_block.start()
    save_search.start()
    for name in GROUPS:
        sent(name)
    save_block.wait()
    save_search.wait()


def body(eigen_block, search_dirs):
    shape = eigen_block.shape
    flat = (shape[0] * shape[1] * shape[2], shape[3])
    vmem = pltpu.VMEM
    fine = (NX + 2 * H, NY + 2 * H, K, NZ)
    rough = (CX + 2 * HC, CY + 2 * HC, K // 2, NZ)
    scratch = [
        vmem(flat, F32),
        vmem(flat, F32),
        vmem(fine, F32),
        vmem((NX + 2, NY + 2, K, NZ), F32),
        vmem((NX + 2, NY + 2, K, NZ), F32),
        vmem(fine, F32),
        vmem(fine, F32),
        vmem(fine, F32),
        vmem(fine, F32),
        vmem(fine, F32),
        vmem(rough, F32),
        vmem(rough, F32),
        vmem(rough, F32),
        vmem((CX + 2 * HD, CY + 2 * HD, K // 2, NZ), F32),
        vmem((NX * NY, 256, NZ), BF16),
        vmem(flat, F32),
        vmem(flat, F32),
        vmem((3, K, NZ), F32),
        vmem((1, K, NZ), F32),
        vmem((15, K, NZ), F32),
        vmem((7, K, NZ), F32),
        vmem((4, 8, NZ), F32),
        vmem((1, 8, NZ), F32),
        vmem((15, 8, NZ), F32),
        vmem((7, 8, NZ), F32),
        vmem((2, 8, NZ), F32),
        pltpu.SemaphoreType.DMA((COUNT,)),
        pltpu.SemaphoreType.DMA((COUNT,)),
        pltpu.SemaphoreType.DMA((47,)),
        pltpu.SemaphoreType.DMA((47,)),
        pltpu.SemaphoreType.DMA((2,)),
    ]
    block, search = pl.pallas_call(
        kernel,
        out_shape=(jax.ShapeDtypeStruct(flat, F32), jax.ShapeDtypeStruct(flat, F32)),
        in_specs=[pl.BlockSpec(memory_space=pl.ANY)] * 2,
        out_specs=(pl.BlockSpec(memory_space=pl.ANY), pl.BlockSpec(memory_space=pl.ANY)),
        scratch_shapes=scratch,
        compiler_params=pltpu.CompilerParams(
            collective_id=0, has_side_effects=True, vmem_limit_bytes=56 * 1024 * 1024
        ),
    )(eigen_block.reshape(flat), search_dirs.reshape(flat))
    return block.reshape(shape), search.reshape(shape)


def solution(mesh):
    spec = P(None, "gx", "gy", None)
    return jax.shard_map(body, mesh=mesh, in_specs=(spec, spec), out_specs=(spec, spec), check_vma=False)
```

```python
import functools

import jax
import jax.numpy as jnp
from jax import lax
from jax.experimental import pallas as pl
from jax.experimental.pallas import tpu as pltpu
from jax.sharding import PartitionSpec as P

MESH = pl.DeviceIdType.MESH
HP = lax.Precision.HIGHEST
F32 = jnp.float32
BF16 = jnp.bfloat16

K = 16
NX, NY, NZ = 8, 16, 128
H = 4
CX, CY = NX // 2, NY // 2
HC = 4
HD = 1
SHIFT = 13.0
X, PD, IX, IP, W, IW = 0, 16, 32, 48, 64, 80

DIRS = [(-1, 0), (1, 0), (0, -1), (0, 1), (-1, -1), (-1, 1), (1, -1), (1, 1)]


def masks_of(bits):
    out = [(0, 0)]
    for bx, by in bits:
        out = out + [(x | bx, y | by) for x, y in out]
    return out[1:]


CORE = masks_of([(1, 0)])
PLANE = masks_of([(2, 0), (0, 1), (4, 0), (8, 0)])
DEPTH = masks_of([(0, 2), (0, 4), (0, 8)])


def span(step, layers, size, offset):
    if step == 0:
        return (offset, offset, size)
    first, last = layers
    count = last - first + 1
    if step < 0:
        return (offset + first - 1, offset + size + first - 1, count)
    return (offset + size - last, offset - last, count)


def transfers():
    groups = {}
    groups["x1"] = [("x", d, (1, 1), (1, 1)) for d in range(4)]
    groups["x2"] = [("x", d, (2, 2), (2, 2)) for d in range(4)] + [("x", d, (1, 1), (1, 1)) for d in range(4, 8)]
    groups["x3"] = [("x", d, (3, 3), (3, 3)) for d in range(4)]
    deep = [("x", d, (4, 4), (4, 4)) for d in range(4)]
    for d in range(4, 8):
        deep += [("x", d, (1, 1), (2, 3)), ("x", d, (2, 2), (1, 2)), ("x", d, (3, 3), (1, 1))]
    groups["x4"] = deep
    groups["p1"] = [("p", d, (1, 1), (1, 1)) for d in (1, 3)]
    groups["w1"] = [("w", d, (1, 1), (1, 1)) for d in (1, 3)]
    rough = [("cr", d, (1, 4), (1, 4)) for d in range(4)]
    for d in range(4, 8):
        rough += [("cr", d, (1, 1), (1, 3)), ("cr", d, (2, 2), (1, 2)), ("cr", d, (3, 3), (1, 1))]
    groups["cr"] = rough
    sums = [("s", d, (3, 3), (3, 3)) for d in range(4)]
    for d in range(4, 8):
        sums += [("s", d, (1, 1), (2, 2)), ("s", d, (2, 2), (1, 1))]
    groups["s"] = sums
    return groups


GROUPS = transfers()
FIRST = {}
COUNT = 0
for _name in GROUPS:
    FIRST[_name] = COUNT
    COUNT += len(GROUPS[_name])

GEOMETRY = {"x": (NX, NY, H), "p": (NX, NY, 1), "w": (NX, NY, 1), "s": (NX, NY, H), "cr": (CX, CY, HC)}


def tree(parts):
    while len(parts) > 1:
        parts = [parts[i] + parts[i + 1] for i in range(0, len(parts), 2)]
    return parts[0]


def chunks(start, stop, width=4):
    return [(j, min(width, stop - j)) for j in range(start, stop, width)]


def kernel(
    x_hbm, p_hbm, block_hbm, search_hbm,
    x_nat, p_nat, x_ext, p_ext, w_ext, r_ext, ea, eb, ec, s_ext, crp, ca, cb, cd, split, out_block, out_search,
    th_mine, th_core, th_plane, th_depth, ar_mine, ar_core, ar_plane, ar_depth, ar_full,
    send_sem, recv_sem, red_send, red_recv, local_sem,
):
    gx, gy = lax.axis_index("gx"), lax.axis_index("gy")
    nx, ny = lax.axis_size("gx"), lax.axis_size("gy")
    core = lax.rem(gx, 2)
    load_x = pltpu.make_async_copy(x_hbm, x_nat, local_sem.at[0])
    load_p = pltpu.make_async_copy(p_hbm, p_nat, local_sem.at[1])
    load_x.start()
    load_p.start()

    buffers = {"x": x_ext, "p": p_ext, "s": s_ext, "cr": crp, "w": w_ext}
    lane = lax.broadcasted_iota(jnp.int32, (1, 1, NZ), 2)
    first_z, last_z, even = lane == 0, lane == NZ - 1, lane % 2 == 0

    def exists(d, sign):
        dx, dy = DIRS[d]
        tests = []
        if dx:
            tests.append(gx > 0 if dx * sign < 0 else gx < nx - 1)
        if dy:
            tests.append(gy > 0 if dy * sign < 0 else gy < ny - 1)
        return functools.reduce(jnp.logical_and, tests)

    def copy_of(name, index):
        key, d, rows, cols = GROUPS[name][index]
        dx, dy = DIRS[d]
        sx, sy, offset = GEOMETRY[key]
        rs, rd, rn = span(dx, rows, sx, offset)
        cs, cd_, cn = span(dy, cols, sy, offset)
        buf = buffers[key]
        sem = FIRST[name] + index
        return d, pltpu.make_async_remote_copy(
            src_ref=buf.at[pl.ds(rs, rn), pl.ds(cs, cn)],
            dst_ref=buf.at[pl.ds(rd, rn), pl.ds(cd_, cn)],
            send_sem=send_sem.at[sem],
            recv_sem=recv_sem.at[sem],
            device_id=(gx + dx, gy + dy),
            device_id_type=MESH,
        )

    def send(name):
        for index in range(len(GROUPS[name])):
            d, copy = copy_of(name, index)
            pl.when(exists(d, 1))(copy.start)

    def receive(name):
        for index in range(len(GROUPS[name])):
            d, copy = copy_of(name, index)
            pl.when(exists(d, -1))(copy.wait_recv)

    def sent(name):
        for index in range(len(GROUPS[name])):
            d, copy = copy_of(name, index)
            pl.when(exists(d, 1))(copy.wait_send)

    def exchange(masks, base, source, slots):
        copies = [
            pltpu.make_async_remote_copy(
                src_ref=source,
                dst_ref=slots.at[i],
                send_sem=red_send.at[base + i],
                recv_sem=red_recv.at[base + i],
                device_id=(gx ^ mx, gy ^ my),
                device_id_type=MESH,
            )
            for i, (mx, my) in enumerate(masks)
        ]
        for copy in copies:
            copy.start()

        def finish():
            for copy in copies:
                copy.wait_send()
                copy.wait_recv()

        return finish

    barrier = pltpu.get_barrier_semaphore()
    partners = CORE + PLANE + DEPTH
    for mx, my in partners:
        pl.semaphore_signal(barrier, inc=1, device_id=(gx ^ mx, gy ^ my), device_id_type=MESH)

    def clear(ref, offset, always=False):
        rows, cols = ref.shape[:2]

        def block(i, j, n, m):
            ref[pl.ds(i, n), pl.ds(j, m)] = jnp.zeros((n, m) + tuple(ref.shape[2:]), ref.dtype)

        def lines(first):
            def line(i, carry):
                block(i, 0, 1, cols)
                return carry
            lax.fori_loop(first, first + offset, line, 0)

        def columns(first):
            def line(i, carry):
                block(i, first, 1, offset)
                return carry
            lax.fori_loop(0, rows, line, 0)

        def where(test, fill, first):
            if always:
                fill(first)
            else:
                pl.when(test)(lambda: fill(first))

        where(gx == 0, lines, 0)
        where(gx == nx - 1, lines, rows - offset)
        where(gy == 0, columns, 0)
        where(gy == ny - 1, columns, cols - offset)

    clear(x_ext, H)
    clear(p_ext, 1, always=True)
    clear(w_ext, 1, always=True)
    clear(s_ext, H)
    clear(crp, HC)

    expected = 0
    for d in range(8):
        dx, dy = DIRS[d]
        there = exists(d, 1)

        @pl.when(there)
        def _():
            pl.semaphore_signal(barrier, inc=1, device_id=(gx + dx, gy + dy), device_id_type=MESH)

        expected = expected + jnp.where(there, 1, 0)


    def put(cell, row, value):
        high = value.astype(BF16)
        split[cell, pl.ds(row, K)] = high
        split[cell, pl.ds(row + 128, K)] = (value - high.astype(F32)).astype(BF16)

    load_x.wait()

    def bring_x(i, carry):
        for j in range(NY):
            value = x_nat[pl.ds(i * NY + j, K, stride=NX * NY), :]
            x_ext[i + H, j + H] = value
        return carry

    lax.fori_loop(0, NX, bring_x, 0)
    pl.semaphore_wait(barrier, expected + len(partners))
    send("x1")
    send("x2")
    send("x3")
    load_p.wait()
    clear(r_ext, H)
    clear(ea, H)
    clear(eb, H)
    clear(ec, H)
    clear(ca, HC)
    clear(cb, HC)
    clear(cd, HD)

    def bring_p(i, carry):
        for j in range(NY):
            p_ext[i + 1, j + 1] = p_nat[pl.ds(i * NY + j, K, stride=NX * NY), :]
        return carry

    lax.fori_loop(0, NX, bring_p, 0)

    def keep(i, carry):
        for j in range(NY):
            cell = i * NY + j
            put(cell, X, x_ext[i + H, j + H])
            put(cell, PD, p_ext[i + 1, j + 1])
            split[cell, pl.ds(96, 32)] = jnp.zeros((32, NZ), BF16)
            split[cell, pl.ds(224, 32)] = jnp.zeros((32, NZ), BF16)
        return carry

    lax.fori_loop(0, NX, keep, 0)

    def beside_z(center, step):
        zero = jnp.zeros_like(center)
        if step == 1:
            down = jnp.where(first_z, zero, pltpu.roll(center, 1, 2))
            up = jnp.where(last_z, zero, pltpu.roll(center, NZ - 1, 2))
        else:
            down = jnp.where(lane < 2, zero, pltpu.roll(center, 2, 2))
            up = jnp.where(lane >= NZ - 2, zero, pltpu.roll(center, NZ - 2, 2))
        return down + up

    def around(ref, i, j, n, step=1):
        line = ref[i, pl.ds(j - 1, n + 2)]
        center = line[1 : n + 1]
        beside = ref[i - 1, pl.ds(j, n)] + ref[i + 1, pl.ds(j, n)]
        beside = beside + (line[0:n] + line[2 : n + 2])
        return center, beside + beside_z(center, step)

    left = jnp.where(gy > 0, 1.0, 0.0).astype(F32)
    right = jnp.where(gy < ny - 1, 1.0, 0.0).astype(F32)

    def sweep(depth, sizes, offset, body, width=4):
        sx, sy = sizes
        low = jnp.where(gx > 0, offset - depth, offset)
        high = jnp.where(gx < nx - 1, offset + sx + depth, offset + sx)

        def row(i, carry):
            if depth:
                body(i, offset - depth, depth, left)
            for j, n in chunks(offset, offset + sy, width):
                body(i, j, n, None)
            if depth:
                body(i, offset + sy, depth, right)
            return carry

        lax.fori_loop(low, high, row, 0)

    def scaled(value, scale):
        return value if scale is None else value * scale

    receive("x1")

    def image_x(i, carry):
        numer, denom = carry
        for j, n in chunks(H, H + NY):
            center, beside = around(x_ext, i + H, j, n)
            image = 6.0 * center - beside
            for q in range(n):
                put(i * NY + j - H + q, IX, image[q])
            numer = numer + jnp.sum(center * image, axis=0)
            denom = denom + jnp.sum(center * center, axis=0)
        return numer, denom

    zero = jnp.zeros((K, NZ), F32)
    numer, denom = lax.fori_loop(0, NX, image_x, (zero, zero))
    numer = jnp.sum(numer, axis=1, keepdims=True)
    denom = jnp.sum(denom, axis=1, keepdims=True)

    def pair(cell, row, count):
        return jnp.concatenate([split[cell, pl.ds(row, count)], split[cell + 1, pl.ds(row, count)]], axis=1)

    def product(lhs, rhs, acc):
        return acc + lax.dot_general(lhs, rhs, (((1,), (1,)), ((), ())), preferred_element_type=F32)

    def early_products(i, acc):
        for j in range(0, NY, 2):
            cell = i * NY + j
            high, low = pair(cell, X, 48), pair(cell, X + 128, 48)
            rhs = jnp.concatenate([high, low], axis=0)
            lhs = jnp.concatenate([high[0:32], low[0:32]], axis=0)
            acc = product(lhs, rhs, acc)
        return acc

    early = lax.fori_loop(0, NX, early_products, jnp.zeros((64, 96), F32))
    early = jnp.concatenate([early[0:32] + early[32:64], jnp.zeros((32, 32), F32)], axis=1)
    early = early + pltpu.roll(early, NZ - 48, 1)
    lane2 = lax.broadcasted_iota(jnp.int32, (K, NZ), 1)
    ratio = jnp.where(lane2 < 112, numer, denom)
    early = jnp.where(lane2 < 48, early[0:16], jnp.where(lane2 < 96, pltpu.roll(early[16:32], 48, 1), ratio))
    th_mine[0] = early
    exchange(CORE, 0, th_mine.at[0], th_core)()
    th_mine[1] = th_mine[0] + th_core[0]
    plane_done = exchange(PLANE, 1, th_mine.at[1], th_plane)
    send("x4")

    receive("x2")

    def power_1(i, j, n, scale):
        center, beside = around(x_ext, i, j, n)
        ea[i, pl.ds(j, n)] = scaled(center * (1.0 / 3.0) + beside * (1.0 / 9.0), scale)

    def cross_line(i):
        for j, n in chunks(H, H + NY):
            power_1(i, j, n, None)

    def cross(i, carry):
        power_1(i, H - 1, 1, left)
        cross_line(i)
        power_1(i, H + NY, 1, right)
        return carry

    lax.fori_loop(H, H + NX, cross, 0)
    pl.when(gx > 0)(lambda: cross_line(H - 1))
    pl.when(gx < nx - 1)(lambda: cross_line(H + NX))

    def sum_inner(i, j, n, scale):
        center, beside = around(ea, i, j, n)
        s_ext[i, pl.ds(j, n)] = x_ext[i, pl.ds(j, n)] + (center * (4.0 / 3.0) + beside * (1.0 / 9.0))

    sweep(0, (NX, NY), H, sum_inner)
    send("s")
    plane_done()
    th_mine[2] = tree([th_mine[1]] + [th_plane[i] for i in range(15)])
    depth_done = exchange(DEPTH, 16, th_mine.at[2], th_depth)

    receive("x3")
    receive("x4")

    def power_2(i, j, n, scale):
        center, beside = around(ea, i, j, n)
        eb[i, pl.ds(j, n)] = scaled(center * (1.0 / 3.0) + beside * (1.0 / 9.0), scale)

    def power_3(i, j, n, scale):
        center, beside = around(eb, i, j, n)
        ec[i, pl.ds(j, n)] = scaled(center * (1.0 / 3.0) + beside * (1.0 / 9.0), scale)

    sweep(3, (NX, NY), H, power_1)
    sweep(2, (NX, NY), H, power_2)
    sweep(1, (NX, NY), H, power_3)
    depth_done()
    total = tree([th_mine[2]] + [th_depth[i] for i in range(7)])
    theta = jnp.broadcast_to(total[:, 96:97] / total[:, 112:113], (K, NZ))
    shifted = 6.0 - theta

    def restrict(ci, carry):
        for j, n in chunks(H, H + NY):
            total = None
            for half in range(2):
                center, beside = around(ec, 2 * ci + half + H, j, n)
                rest = shifted * center - beside
                total = rest if total is None else total + rest
            for q in range(0, n, 2):
                cube = total[q] + total[q + 1]
                low, high = cube[0:8], cube[8:16]
                low = low + pltpu.roll(low, NZ - 1, 1)
                high = high + pltpu.roll(high, 1, 1)
                crp[ci + HC, (j - H + q) // 2 + HC] = jnp.where(even[0], low, high)
        return carry

    lax.fori_loop(0, CX, restrict, 0)
    send("cr")

    def sum_outer(i, j, n):
        s_ext[i, pl.ds(j, n)] = x_ext[i, pl.ds(j, n)] + ea[i, pl.ds(j, n)] + eb[i, pl.ds(j, n)]

    def sum_sides(i, carry):
        sum_outer(i, H - 2, 2)
        sum_outer(i, H + NY, 2)
        return carry

    lax.fori_loop(H, H + NX, sum_sides, 0)
    for i in (H - 2, H - 1, H + NX, H + NX + 1):
        for j, n in chunks(H, H + NY):
            sum_outer(i, j, n)
    for i in (H - 1, H + NX):
        sum_outer(i, H - 1, 1)
        sum_outer(i, H + NY, 1)
    receive("s")

    def second_sweep(i, j, n, scale):
        center, beside = around(s_ext, i, j, n)
        ec[i, pl.ds(j, n)] = scaled((shifted * center - beside) * (1.0 / 9.0), scale)

    sweep(2, (NX, NY), H, second_sweep)

    def residual(i, j, n, scale):
        center, beside = around(x_ext, i, j, n)
        r_ext[i, pl.ds(j, n)] = scaled(shifted * center - beside, scale)

    sweep(2, (NX, NY), H, residual)

    def smoothed(source, i, j, n):
        center, beside = around(source, i, j, n)
        return center * (1.0 / 3.0) + (r_ext[i, pl.ds(j, n)] + beside) * (1.0 / 9.0)

    def inverse_factor(matrix, size):
        rows = lax.broadcasted_iota(jnp.int32, (size, NZ), 0)
        lanes = lax.broadcasted_iota(jnp.int32, (size, NZ), 1)
        start = jnp.where(lanes < size, matrix, jnp.where(lanes == rows + 64, 1.0, 0.0))
        tiles = [start[8 * t : 8 * t + 8] for t in range(size // 8)]
        sub = lax.broadcasted_iota(jnp.int32, (8, NZ), 0)
        for k in range(size):
            t0, s0 = k // 8, k % 8
            pivot = tiles[t0][s0 : s0 + 1]
            pivot = pivot / pivot[:, k : k + 1]
            for t in range(t0, size // 8):
                column = jnp.broadcast_to(tiles[t][:, k : k + 1], (8, NZ))
                if t == t0:
                    column = jnp.where(sub > s0, column, 0.0)
                tiles[t] = tiles[t] - column * pivot
        done = jnp.concatenate(tiles, axis=0)
        diagonal = jnp.sum(jnp.where(lanes == rows, done, 0.0), axis=1, keepdims=True)
        return pltpu.roll(done / jnp.sqrt(diagonal), 64, 1)[:, 0:size]

    def dot(a, b):
        return jnp.dot(a, b, precision=HP, preferred_element_type=F32)

    def dot_t(a, b):
        return lax.dot_general(a, b, (((1,), (1,)), ((), ())), precision=HP, preferred_element_type=F32)

    def moved(value, start, end):
        return pltpu.roll(value, (end - start) % NZ, 1) if start != end else value

    first_inv = inverse_factor(jnp.concatenate([total, moved(total, 48, 0)], axis=0), 32)

    receive("cr")
    send("p1")

    def coarse_first(i, j, n, scale):
        center, beside = around(crp, i, j, n, 2)
        ca[i, pl.ds(j, n)] = scaled(center * (1.0 / 27.0) + beside * (1.0 / 324.0), scale)

    def coarse_next(source, target, shift):
        def body(i, j, n, scale):
            center, beside = around(source, i, j, n, 2)
            value = center * (1.0 / 3.0) + crp[i, pl.ds(j, n)] * (1.0 / 36.0) + beside * (1.0 / 9.0)
            target[i - shift, pl.ds(j - shift, n)] = scaled(value, scale)
        return body

    sweep(3, (CX, CY), HC, coarse_first)
    sweep(2, (CX, CY), HC, coarse_next(ca, cb, 0))
    sweep(1, (CX, CY), HC, coarse_next(cb, cd, HC - HD))
    def correct(ci, carry):
        for cj in range(CY + 2 * HD):
            packed = cd[ci, cj]
            low = jnp.where(even[0], packed, pltpu.roll(packed, 1, 1))
            high = jnp.where(even[0], pltpu.roll(packed, NZ - 1, 1), packed)
            both = jnp.concatenate([low, high], axis=0)
            for half in range(2):
                i, j = 2 * (ci - HD) + half + H, 2 * (cj - HD) + H
                ea[i, pl.ds(j, 2)] = ec[i, pl.ds(j, 2)] + both[None]
        return carry

    lax.fori_loop(0, CX + 2 * HD, correct, 0)

    def third_sweep(i, j, n, scale):
        eb[i, pl.ds(j, n)] = scaled(smoothed(ea, i, j, n), scale)

    def fourth_sweep(i, j, n, scale):
        value = smoothed(eb, i, j, n)
        w_ext[i - H + 1, pl.ds(j - H + 1, n)] = value
        for q in range(n):
            put((i - H) * NY + j - H + q, W, value[q])

    sweep(1, (NX, NY), H, third_sweep)
    sweep(0, (NX, NY), H, fourth_sweep)
    send("w1")

    def half_image(ref, row):
        def double(i, carry):
            ref[i, 0] = ref[i, 0] * 2.0
            return carry

        lax.fori_loop(1, 1 + NX, double, 0)
        for j, n in chunks(1, 1 + NY):
            ref[0, pl.ds(j, n)] = ref[0, pl.ds(j, n)] * 2.0

        def image_row(i, carry):
            for j, n in chunks(1, 1 + NY):
                center, beside = around(ref, i + 1, j, n)
                image = 6.0 * center - beside
                for q in range(n):
                    put(i * NY + j - 1 + q, row, image[q])
            return carry

        lax.fori_loop(0, NX, image_row, 0)

    receive("p1")
    half_image(p_ext, IP)

    def late_products(i, acc):
        for j in range(0, NY, 2):
            cell = i * NY + j
            high, low = pair(cell, X, 80), pair(cell, X + 128, 80)
            rhs = jnp.concatenate([high[48:80], low[48:80]], axis=0)
            acc = product(jnp.concatenate([high, low], axis=0), rhs, acc)
        return acc

    late = lax.fori_loop(0, NX, late_products, jnp.zeros((160, 64), F32))
    receive("w1")
    half_image(w_ext, IW)

    def last_products(i, acc):
        for j in range(0, NY, 2):
            cell = i * NY + j
            rhs = jnp.concatenate([pair(cell, IW, 16), pair(cell, IW + 128, 16)], axis=0)
            lhs = [pair(cell, row, 16) for row in (PD, W, PD + 128, W + 128)]
            acc = product(jnp.concatenate(lhs, axis=0), rhs, acc)
        return acc

    last = lax.fori_loop(0, NX, last_products, jnp.zeros((64, 32), F32))

    def folded(value, half, width):
        value = value[0:half] + value[half : 2 * half]
        value = jnp.concatenate([value, jnp.zeros((half, NZ - 2 * width), F32)], axis=1)
        return value + pltpu.roll(value, NZ - width, 1)

    late = folded(late, 80, 32)
    last = folded(last, 32, 16)

    mixed = 0.5 * (moved(late[48:64], 16, 48) + moved(last[0:16], 0, 48))
    blocks = [
        moved(late[0:16], 16, 0),
        late[32:48],
        moved(late[16:32], 16, 32),
        mixed,
        moved(late[64:80], 16, 64),
        moved(last[16:32], 0, 80),
        moved(late[16:32], 0, 96),
    ]
    part = jnp.zeros((K, NZ), F32)
    for index, block in enumerate(blocks):
        part = jnp.where(lane2 // K == index, block, part)
    ar_mine[0] = part[0:8]
    ar_mine[1] = part[8:16]
    exchange(CORE, 23, ar_mine.at[1 - core], ar_core)()
    ar_mine[2] = ar_mine[core] + ar_core[0]
    exchange(PLANE, 24, ar_mine.at[2], ar_plane)()
    ar_mine[3] = tree([ar_mine[2]] + [ar_plane[i] for i in range(15)])
    exchange(DEPTH, 39, ar_mine.at[3], ar_depth)()
    ar_full[core] = tree([ar_mine[3]] + [ar_depth[i] for i in range(7)])
    swap = pltpu.make_async_remote_copy(
        src_ref=ar_full.at[core],
        dst_ref=ar_full.at[core],
        send_sem=red_send.at[46],
        recv_sem=red_recv.at[46],
        device_id=(gx ^ 1, gy),
        device_id_type=MESH,
    )
    swap.start()
    swap.wait_send()
    swap.wait_recv()

    both = jnp.concatenate([ar_full[0], ar_full[1]], axis=0)

    rows = lax.broadcasted_iota(jnp.int32, (48, 48), 0)
    cols = lax.broadcasted_iota(jnp.int32, (48, 48), 1)

    def upper(first, second, third):
        return jnp.concatenate([first, second, third], axis=0)[:, 0:48]

    x_rows, p_rows = total, moved(total, 48, 0)
    proj = upper(
        jnp.where(lane2 < 32, moved(x_rows, 32, 0), moved(both, 16, 32)),
        jnp.where(lane2 < 16, moved(p_rows, 32, 0), jnp.where(lane2 < 32, moved(both, 96, 16), moved(both, 48, 32))),
        moved(both, 80, 32),
    )
    below = jnp.logical_and(rows >= 32, cols < 32)
    beside_x = jnp.logical_and(rows < 16, jnp.logical_and(cols >= 16, cols < 32))
    proj = jnp.where(jnp.logical_or(below, beside_x), proj.T, proj)
    proj = 0.5 * (proj + proj.T)
    with_w = jnp.concatenate([both, moved(both, 32, 0)], axis=0)[:, 0:K]
    below_t = dot(first_inv, with_w).T
    schur = moved(both, 64, 0)[:, 0:K] - dot_t(below_t, below_t)
    last_inv = inverse_factor(jnp.concatenate([schur, jnp.zeros((K, NZ - K), F32)], axis=1), K)
    corner = dot(last_inv, dot(below_t, first_inv))
    lower_inv = jnp.concatenate(
        [
            jnp.concatenate([first_inv, jnp.zeros((32, K), F32)], axis=1),
            jnp.concatenate([-corner, last_inv], axis=1),
        ],
        axis=0,
    )
    ritz = dot_t(dot(lower_inv, proj), lower_inv)
    ritz = 0.5 * (ritz + ritz.T)
    rows = lax.broadcasted_iota(jnp.int32, (K, 48), 0)
    cols = lax.broadcasted_iota(jnp.int32, (K, 48), 1)
    filtered_t = jnp.where(rows == cols, SHIFT, 0.0) - ritz[0:K]
    square = dot_t(filtered_t, filtered_t)
    square = jnp.concatenate([square, jnp.zeros((K, NZ - K), F32)], axis=1)
    small_inv = inverse_factor(square, K)
    ncells = float(NX * NY * NZ * nx * ny)
    coef_t = dot(dot(small_inv, filtered_t), lower_inv) * (ncells**0.5)

    coef_t = jnp.concatenate([coef_t, jnp.where(cols < K, 0.0, coef_t)], axis=0)
    gap = jnp.zeros((2 * K, 32), F32)
    coef_t = jnp.concatenate([coef_t[:, 0:32], gap, coef_t[:, 32:48], gap, gap[:, 0:16]], axis=1)
    high = coef_t.astype(BF16)
    low = (coef_t - high.astype(F32)).astype(BF16)
    weights = jnp.concatenate([high, low], axis=0)
    weights = jnp.concatenate([weights, weights], axis=1)

    def combine(i, carry):
        for j in range(0, NY, 2):
            cell = i * NY + j
            rhs = jnp.concatenate([split[cell], split[cell + 1]], axis=1)
            out = jnp.dot(weights, rhs, preferred_element_type=F32)
            out = out[0:32] + out[32:64]
            for q in range(2):
                out_block[pl.ds(cell + q, K, stride=NX * NY), :] = out[0:16, 128 * q : 128 * q + 128]
                out_search[pl.ds(cell + q, K, stride=NX * NY), :] = out[16:32, 128 * q : 128 * q + 128]
        return carry

    lax.fori_loop(0, NX, combine, 0)
    save_block = pltpu.make_async_copy(out_block, block_hbm, local_sem.at[0])
    save_search = pltpu.make_async_copy(out_search, search_hbm, local_sem.at[1])
    save_block.start()
    save_search.start()
    for name in GROUPS:
        sent(name)
    save_block.wait()
    save_search.wait()


def body(eigen_block, search_dirs):
    shape = eigen_block.shape
    flat = (shape[0] * shape[1] * shape[2], shape[3])
    vmem = pltpu.VMEM
    fine = (NX + 2 * H, NY + 2 * H, K, NZ)
    rough = (CX + 2 * HC, CY + 2 * HC, K // 2, NZ)
    scratch = [
        vmem(flat, F32),
        vmem(flat, F32),
        vmem(fine, F32),
        vmem((NX + 2, NY + 2, K, NZ), F32),
        vmem((NX + 2, NY + 2, K, NZ), F32),
        vmem(fine, F32),
        vmem(fine, F32),
        vmem(fine, F32),
        vmem(fine, F32),
        vmem(fine, F32),
        vmem(rough, F32),
        vmem(rough, F32),
        vmem(rough, F32),
        vmem((CX + 2 * HD, CY + 2 * HD, K // 2, NZ), F32),
        vmem((NX * NY, 256, NZ), BF16),
        vmem(flat, F32),
        vmem(flat, F32),
        vmem((3, K, NZ), F32),
        vmem((1, K, NZ), F32),
        vmem((15, K, NZ), F32),
        vmem((7, K, NZ), F32),
        vmem((4, 8, NZ), F32),
        vmem((1, 8, NZ), F32),
        vmem((15, 8, NZ), F32),
        vmem((7, 8, NZ), F32),
        vmem((2, 8, NZ), F32),
        pltpu.SemaphoreType.DMA((COUNT,)),
        pltpu.SemaphoreType.DMA((COUNT,)),
        pltpu.SemaphoreType.DMA((47,)),
        pltpu.SemaphoreType.DMA((47,)),
        pltpu.SemaphoreType.DMA((2,)),
    ]
    block, search = pl.pallas_call(
        kernel,
        out_shape=(jax.ShapeDtypeStruct(flat, F32), jax.ShapeDtypeStruct(flat, F32)),
        in_specs=[pl.BlockSpec(memory_space=pl.ANY)] * 2,
        out_specs=(pl.BlockSpec(memory_space=pl.ANY), pl.BlockSpec(memory_space=pl.ANY)),
        scratch_shapes=scratch,
        compiler_params=pltpu.CompilerParams(
            collective_id=0, has_side_effects=True, vmem_limit_bytes=56 * 1024 * 1024
        ),
    )(eigen_block.reshape(flat), search_dirs.reshape(flat))
    return block.reshape(shape), search.reshape(shape)


def solution(mesh):
    spec = P(None, "gx", "gy", None)
    return jax.shard_map(body, mesh=mesh, in_specs=(spec, spec), out_specs=(spec, spec), check_vma=False)
```
